32 devices in a mesh: row: 4 (over y, core), col: 8 (over z, x).
Axes of the slice: x: 2, y: 2, z: 4, core: 2. Of those that a mesh axis runs over, the one named last changes fastest.
Arguments:
- features: float32 [128, 512, 128], P('row', 'col'), may hold values from -0.4 to 0.4
- step_size: float32 [128, 512, 128], P('row', 'col'), may hold values from 0.5 to 2
- write_weights: float32 [128, 512, 16], P('row', 'col'), may hold values from -6 to 6
- read_weights: float32 [128, 512, 16], P('row', 'col'), may hold values from -6 to 6
- decay_log: float32 [16, 128], replicated, may hold values from -7.6 to -3.5
- out_grad: float32 [128, 512, 128], P('row', 'col'), may hold values from -0.4 to 0.4
Outputs:
- grad_features: float32 [128, 512, 128], P('row', 'col')
- grad_step: float32 [128, 512, 128], P('row', 'col')
- grad_write: float32 [128, 512, 16], P('row', 'col')
- grad_read: float32 [128, 512, 16], P('row', 'col')
- grad_decay: float32 [16, 128], replicated
The draws below stay inside these ranges and needn't reach their ends.
All inputs are finite; a program needn't handle non-finite values.
Results may differ from the reference program's by a relative error of at most 0.0002.
Values sent between devices are 32-bit elements; how exact they have to be, the bound alone decides.
No kernel may reach another device: no remote copies, remote signals or barrier semaphores. Data moves between devices by JAX's collectives and lax.ppermute only.
A program may use at most 320 MiB of HBM per device.

```python
import math
import jax
import jax.numpy as jnp
from jax import lax

D = 128
NS = 16
H = 128
W = 512


def shard_levels(stream_key, extent, split, low, largest):
    def one(axis_at, blocks):
        steps = jax.random.uniform(jax.random.fold_in(jax.random.fold_in(stream_key, 6), axis_at), (blocks,), jnp.float32, low / len(split), largest / len(split))
        return jnp.repeat(jnp.exp(steps), extent[axis_at] // blocks).reshape((-1,) + (1,) * (len(extent) - axis_at - 1))

    loudness = one(*split[0])
    for cut in split[1:]:
        loudness = loudness * one(*cut)
    return loudness


def gaussian(rng, dims, spread, bound, cuts=(), kind=jnp.bfloat16):
    result = spread * jax.random.normal(rng, dims, jnp.float32)
    if cuts:
        result = result * shard_levels(rng, dims, cuts, -0.22, 0.18)
    return jnp.clip(result, -bound, bound).astype(kind)


def setup_inputs(seed: int = 0) -> dict:
    keys = jax.random.split(jax.random.key(seed), 7)
    features = gaussian(keys[0], (H, W, D), 0.05, 0.4, ((0, 4), (1, 8)), jnp.float32)
    step_size = jnp.clip(jnp.exp(math.log(2.0) - 1.3862944 * jax.random.uniform(keys[1], (H, W, D), jnp.float32) ** shard_levels(keys[1], (H, W, D), ((0, 4), (1, 8)), -0.2, 0.2)), 0.5, 2.0)
    write_weights = gaussian(keys[2], (H, W, NS), 1.0, 6.0, ((0, 4), (1, 8)), jnp.float32)
    read_weights = gaussian(keys[3], (H, W, NS), 1.0, 6.0, ((0, 4), (1, 8)), jnp.float32)
    decay_log = jnp.clip(jax.random.uniform(keys[4], (NS, D), jnp.float32, -7.6, -3.5), -7.6, -3.5)
    out_grad = gaussian(keys[5], (H, W, D), 0.05, 0.4, ((0, 4), (1, 8)), jnp.float32)
    return {"features": features, "step_size": step_size, "write_weights": write_weights, "read_weights": read_weights, "decay_log": decay_log, "out_grad": out_grad}


def run_forward(decays, driving):
    def advance(current, inputs):
        factor, source = inputs
        current = factor * current + source
        return current, current
    _, states = lax.scan(advance, jnp.zeros(decays.shape[1:], jnp.float32), (decays, driving))
    return states


def run_backward(decays, driving):
    def retreat(passed, inputs):
        factor, source = inputs
        adjoint = source + passed
        return factor * adjoint, adjoint
    _, adjoints = lax.scan(retreat, jnp.zeros(decays.shape[1:], jnp.float32), (decays, driving), reverse=True)
    return adjoints


def transpose_grid(array):
    return jnp.swapaxes(array, 0, 1)


def reference(features, step_size, write_weights, read_weights, decay_log, out_grad):
    decay_rate = -jnp.exp(decay_log)
    write_by_state = jnp.moveaxis(write_weights, 2, 0)
    read_by_state = jnp.moveaxis(read_weights, 2, 0)
    source_base = step_size * features

    def one_state(carried, inputs):
        through, rate_term = carried
        rate_row, write_plane, read_plane = inputs
        decays = jnp.exp(step_size * rate_row[None, None, :])
        driving = source_base * write_plane[:, :, None]
        vertical = run_forward(decays, driving)
        states = transpose_grid(run_forward(transpose_grid(decays), transpose_grid(vertical)))
        direct = read_plane[:, :, None] * out_grad
        adjoint_h = transpose_grid(run_backward(transpose_grid(decays), transpose_grid(direct)))
        adjoint_v = run_backward(decays, adjoint_h)
        states_prev = jnp.concatenate([jnp.zeros_like(states[:, :1]), states[:, :-1]], 1)
        vert_prev = jnp.concatenate([jnp.zeros_like(vertical[:1]), vertical[:-1]], 0)
        exponent_grad = (adjoint_h * states_prev + adjoint_v * vert_prev) * decays
        through = through + adjoint_v * write_plane[:, :, None]
        rate_term = rate_term + exponent_grad * rate_row[None, None, :]
        write_col = jnp.sum(adjoint_v * source_base, axis=2)
        read_col = jnp.sum(states * out_grad, axis=2)
        decay_row = jnp.sum(exponent_grad * step_size, axis=(0, 1)) * rate_row
        return (through, rate_term), (write_col, read_col, decay_row)

    start = (jnp.zeros(features.shape, jnp.float32), jnp.zeros(features.shape, jnp.float32))
    (through, rate_term), (write_cols, read_cols, grad_decay) = lax.scan(
        one_state, start, (decay_rate, write_by_state, read_by_state))
    grad_features = step_size * through
    grad_step = features * through + rate_term
    grad_write = jnp.moveaxis(write_cols, 0, 2)
    grad_read = jnp.moveaxis(read_cols, 0, 2)
    return grad_features, grad_step, grad_write, grad_read, grad_decay
```

```python
import functools

import jax
import jax.numpy as jnp
import numpy as np
from jax import lax
from jax.experimental import pallas as pl
from jax.experimental.pallas import tpu as pltpu
from jax.sharding import PartitionSpec as P

HS, WS, BI, BJ = 8, 16, 4, 4
POS = BI * BJ
LANES = 128
D = 128
F32 = jnp.float32
BF16 = jnp.bfloat16
LOG2E = 1.4426950408889634
LN2 = 0.6931471805599453


def lane_matrices():
    lane = np.arange(LANES)
    hs, ws = lane // WS, lane % WS
    same_w = ws[:, None] == ws[None]
    same_h = hs[:, None] == hs[None]
    above = same_w & (hs[:, None] < hs[None])
    below = same_w & (hs[:, None] > hs[None])
    left = same_h & (ws[:, None] < ws[None])
    right = same_h & (ws[:, None] > ws[None])
    rows_out = np.stack([
        np.stack([(g * 64 + j * WS + ws)[:, None] == lane[None] for j in range(BJ)])
        for g in range(2)
    ])
    cols_out = np.stack([
        np.stack([(g * 32 + i * HS + hs)[:, None] == lane[None] for i in range(BI)])
        for g in range(4)
    ])
    rows_in = np.swapaxes(rows_out, -1, -2)
    cols_in = np.swapaxes(cols_out, -1, -2)

    def twice(m):
        return jnp.asarray(np.concatenate([m, m], -2).astype(np.float32), BF16)

    return {
        "above": twice(above), "below": twice(below), "left": twice(left), "right": twice(right),
        "rows_out": twice(rows_out), "cols_out": twice(cols_out),
        "rows_in": twice(rows_in), "cols_in": twice(cols_in),
    }


def halves(x):
    high = x.astype(BF16)
    low = (x - high.astype(F32)).astype(BF16)
    return high, low


def lane_dot(x, matrix):
    return jnp.dot(jnp.concatenate(halves(x), 1), matrix, preferred_element_type=F32)


def lane_dot_exact(x, matrix):
    high, low = halves(x)
    rest = (x - high.astype(F32) - low.astype(F32)).astype(BF16)
    return jnp.dot(
        jnp.concatenate([high, low], 1), matrix, preferred_element_type=F32
    ) + jnp.dot(rest, matrix[:LANES], preferred_element_type=F32)


def gather_place(ref, i, j):
    return jnp.concatenate(
        [ref[hs * BI + i, pl.ds(j, WS, stride=BJ), :] for hs in range(HS)], 0
    )


def row_of(ref, p, n):
    return jnp.broadcast_to(ref[p, pl.ds(n, 1), :], (8, LANES))


def forward_rows_kernel(
    step, feat, write, rates, rates_pk, above, left, rows_out, cols_out,
    step_p, source_p, write_p, cum_rows, cum_cols, sum_rows, sum_cols, seg, leaving,
):
    states = rates.shape[0]
    for i in range(BI):
        for j in range(BJ):
            p = i * BJ + j
            s = gather_place(step, i, j).T
            step_p[p] = s
            source_p[p] = s * gather_place(feat, i, j).T
            write_p[p] = gather_place(write, i, j).T
    total = jnp.zeros((64, LANES), F32)
    for j in range(BJ):
        run = [step_p[j]]
        for i in range(1, BI):
            run.append(run[-1] + step_p[i * BJ + j])
        before = lane_dot_exact(run[-1], above[...])
        for i in range(BI):
            cum_rows[i * BJ + j] = before + run[i]
        for g in range(2):
            total += lane_dot_exact(run[-1][g * 64 : g * 64 + 64], rows_out[g, j])
    sum_rows[...] = total
    total = jnp.zeros((32, LANES), F32)
    for i in range(BI):
        run = [step_p[i * BJ]]
        for j in range(1, BJ):
            run.append(run[-1] + step_p[i * BJ + j])
        before = lane_dot_exact(run[-1], left[...])
        for j in range(BJ):
            cum_cols[i * BJ + j] = before + run[j]
        for g in range(4):
            total += lane_dot_exact(run[-1][g * 32 : g * 32 + 32], cols_out[g, i])
    sum_cols[...] = total

    def group(at, carry):
        d = pl.ds(pl.multiple_of((at // (states // 4)) * 8, 8), 8)
        for k in range(4):
            n = (at % (states // 4)) * 4 + k
            r = -rates[n, d]
            for j in range(BJ):
                acc = None
                for i in range(BI):
                    p = i * BJ + j
                    term = jnp.exp2(cum_rows[p, d] * r) * source_p[p, d] * row_of(write_p, p, n)
                    acc = term if acc is None else acc + term
                seg[n, j, d] = acc
        return carry

    lax.fori_loop(0, D // 8 * (states // 4), group, 0)

    for j in range(BJ):
        for g in range(2):
            part = seg[:, j, g * 64 : g * 64 + 64, :].reshape(states * 64, LANES)
            out = lane_dot(part, rows_out[g, j]).reshape(states, 64, LANES)
            if j == 0 and g == 0:
                leaving[...] = out
            else:
                leaving[...] += out
    for n in range(states):
        leaving[n] = leaving[n] * jnp.exp2(rates_pk[n] * sum_rows[...])


def adjoint_cols_kernel(
    grad, read, rates, cum_cols, cols_out, grad_p, read_p, seg, leaving,
):
    states = rates.shape[0]
    for i in range(BI):
        for j in range(BJ):
            p = i * BJ + j
            grad_p[p] = gather_place(grad, i, j).T
            read_p[p] = gather_place(read, i, j).T

    def group(at, carry):
        d = pl.ds(pl.multiple_of((at // (states // 4)) * 8, 8), 8)
        for k in range(4):
            n = (at % (states // 4)) * 4 + k
            r = rates[n, d]
            for i in range(BI):
                acc = None
                for j in range(BJ):
                    p = i * BJ + j
                    term = jnp.exp2(cum_cols[p, d] * r) * grad_p[p, d] * row_of(read_p, p, n)
                    acc = term if acc is None else acc + term
                seg[n, i, d] = acc
        return carry

    lax.fori_loop(0, D // 8 * (states // 4), group, 0)

    for i in range(BI):
        for g in range(4):
            part = seg[:, i, g * 32 : g * 32 + 32, :].reshape(states * 32, LANES)
            out = lane_dot(part, cols_out[g, i]).reshape(states, 32, LANES)
            if i == 0 and g == 0:
                leaving[...] = out
            else:
                leaving[...] += out


def spread(states, blocks, rows, seg, entering, order, enter, scale, out):
    for k in range(seg.shape[1]):
        for g in range(blocks):
            at = pl.ds(g * rows, rows)
            part = seg[:, k, at, :].reshape(states * rows, LANES)
            whole = lane_dot(part, order) + lane_dot(
                entering[...].reshape(states * rows, LANES), enter[g, k]
            )
            out[:, k, at, :] = whole.reshape(states, rows, LANES)
    def rescale(at, carry):
        n, d = at // (D // 8), pl.ds(pl.multiple_of((at % (D // 8)) * 8, 8), 8)
        for k in range(seg.shape[1]):
            out[n, k, d] = out[n, k, d] * scale(n, k, d)
        return carry
    lax.fori_loop(0, states * (D // 8), rescale, 0)


def forward_cols_kernel(
    seg_rows, entering, step_p, source_p, write_p, rates, rates_pk, cum_rows, cum_cols, sum_cols,
    above, rows_in, cols_out, start_rows, seg, leaving,
):
    states = rates.shape[0]
    spread(
        states, 2, 64, seg_rows, entering, above[...], rows_in,
        lambda n, j, d: jnp.exp2(rates[n, d] * (cum_rows[j, d] - step_p[j, d])), start_rows,
    )

    def group(at, carry):
        d = pl.ds(pl.multiple_of((at // (states // 4)) * 8, 8), 8)
        for k in range(4):
            n = (at % (states // 4)) * 4 + k
            r = rates[n, d]
            vert = [start_rows[n, j, d] for j in range(BJ)]
            for i in range(BI):
                state = None
                for j in range(BJ):
                    p = i * BJ + j
                    decay = jnp.exp2(step_p[p, d] * r)
                    vert[j] = decay * vert[j] + source_p[p, d] * row_of(write_p, p, n)
                    state = vert[j] if state is None else decay * state + vert[j]
                seg[n, i, d] = state * jnp.exp2(-r * cum_cols[i * BJ + BJ - 1, d])
        return carry

    lax.fori_loop(0, D // 8 * (states // 4), group, 0)
    for i in range(BI):
        for g in range(4):
            part = seg[:, i, g * 32 : g * 32 + 32, :].reshape(states * 32, LANES)
            out = lane_dot(part, cols_out[g, i]).reshape(states, 32, LANES)
            if i == 0 and g == 0:
                leaving[...] = out
            else:
                leaving[...] += out
    for n in range(states):
        leaving[n] = leaving[n] * jnp.exp2(rates_pk[n] * sum_cols[...])


def adjoint_rows_kernel(
    seg_cols, entering, step_p, grad_p, read_p, rates, rates_pk, cum_rows, cum_cols, sum_cols,
    right, cols_in, rows_out, start_cols, seg, leaving,
):
    states = rates.shape[0]
    for n in range(states):
        leaving[n, 0:32] = entering[n] * jnp.exp2(rates_pk[n] * sum_cols[...])
    spread(
        states, 4, 32, seg_cols, leaving.at[:, 0:32], right[...], cols_in,
        lambda n, i, d: jnp.exp2(-rates[n, d] * cum_cols[i * BJ + BJ - 1, d]), start_cols,
    )

    def group(at, carry):
        d = pl.ds(pl.multiple_of((at // (states // 4)) * 8, 8), 8)
        for k in range(4):
            n = (at % (states // 4)) * 4 + k
            r = rates[n, d]
            passed_v = [None] * BJ
            for i in reversed(range(BI)):
                passed = start_cols[n, i, d]
                for j in reversed(range(BJ)):
                    p = i * BJ + j
                    decay = jnp.exp2(step_p[p, d] * r)
                    adjoint = grad_p[p, d] * row_of(read_p, p, n) + passed
                    passed = decay * adjoint
                    if passed_v[j] is None:
                        passed_v[j] = passed
                    else:
                        passed_v[j] = decay * (adjoint + passed_v[j])
            for j in range(BJ):
                seg[n, j, d] = passed_v[j] * jnp.exp2(r * (cum_rows[j, d] - step_p[j, d]))
        return carry

    lax.fori_loop(0, D // 8 * (states // 4), group, 0)
    for j in range(BJ):
        for g in range(2):
            part = seg[:, j, g * 64 : g * 64 + 64, :].reshape(states * 64, LANES)
            out = lane_dot(part, rows_out[g, j]).reshape(states, 64, LANES)
            if j == 0 and g == 0:
                leaving[...] = out
            else:
                leaving[...] += out


def final_kernel(
    start_rows, start_cols, seg_s, enter_s, seg_v, enter_v,
    step_p, source_p, grad_p, write_p, read_p, rates, rates_v, cum_rows, cum_cols, sum_rows,
    left, below, rows_in, cols_in,
    grad_features, grad_step, grad_write, grad_read, grad_decay,
    in_s, in_v, scaled_v, through, rate_term, sum_w, sum_r, decay_term,
):
    states = rates.shape[0]
    spread(
        states, 4, 32, seg_s, enter_s, left[...], cols_in,
        lambda n, i, d: jnp.exp2(rates[n, d] * (cum_cols[i * BJ, d] - step_p[i * BJ, d])), in_s,
    )
    for n in range(states):
        scaled_v[n] = enter_v[n] * jnp.exp2(rates_v[n] * sum_rows[...])
    spread(
        states, 2, 64, seg_v, scaled_v, below[...], rows_in,
        lambda n, j, d: jnp.exp2(-rates[n, d] * cum_rows[(BI - 1) * BJ + j, d]), in_v,
    )
    sum_w[...] = jnp.zeros_like(sum_w)
    sum_r[...] = jnp.zeros_like(sum_r)

    def block(at, carry):
        d = pl.ds(pl.multiple_of(at * 8, 8), 8)
        for p in range(POS):
            through[p, d] = jnp.zeros((8, LANES), F32)
            rate_term[p, d] = jnp.zeros((8, LANES), F32)

        def one(n, carry):
            r = rates[n, d]
            vert = [start_rows[n, j, d] for j in range(BJ)]
            exps, decays, from_v, from_s = [], [], [], []
            for i in range(BI):
                state = in_s[n, i, d]
                for j in range(BJ):
                    p = i * BJ + j
                    m = step_p[p, d] * r
                    decay = jnp.exp2(m)
                    dv = decay * vert[j]
                    vert[j] = dv + source_p[p, d] * row_of(write_p, p, n)
                    ds = decay * state
                    state = ds + vert[j]
                    sum_r[p, n] += state * grad_p[p, d]
                    exps.append(m)
                    decays.append(decay)
                    from_v.append(dv)
                    from_s.append(ds)
            passed_v = [in_v[n, j, d] for j in range(BJ)]
            total = None
            for i in reversed(range(BI)):
                passed = start_cols[n, i, d]
                for j in reversed(range(BJ)):
                    p = i * BJ + j
                    adjoint = grad_p[p, d] * row_of(read_p, p, n) + passed
                    passed = decays[p] * adjoint
                    adjoint_v = adjoint + passed_v[j]
                    passed_v[j] = decays[p] * adjoint_v
                    q = (adjoint * from_s[p] + adjoint_v * from_v[p]) * exps[p]
                    total = q if total is None else total + q
                    rate_term[p, d] += q
                    through[p, d] += adjoint_v * row_of(write_p, p, n)
                    sum_w[p, n] += adjoint_v * source_p[p, d]
            decay_term[n, d] = total
            return carry

        lax.fori_loop(0, states, one, 0)
        for p in range(POS):
            t = through[p, d]
            s = step_p[p, d]
            rate_term[p, d] = (source_p[p, d] * t + rate_term[p, d] * LN2) / s
            through[p, d] = s * t
        return carry

    lax.fori_loop(0, D // 8, block, 0)
    for i in range(BI):
        for j in range(BJ):
            p = i * BJ + j
            for values, out in ((through, grad_features), (rate_term, grad_step)):
                back = values[p].T
                for hs in range(HS):
                    out[hs * BI + i, pl.ds(j, WS, stride=BJ), :] = back[hs * WS : hs * WS + WS]
            grad_write[p] = jnp.sum(sum_w[p], 1)
            grad_read[p] = jnp.sum(sum_r[p], 1)
    ones = jnp.ones((8, 2 * LANES), BF16)
    for n in range(states):
        part = jnp.concatenate(halves(decay_term[n]), 1)
        out = lax.dot_general(ones, part, (((1,), (1,)), ((), ())), preferred_element_type=F32)
        grad_decay[pl.ds(n, 1)] = out[0:1] * LN2


def run(kernel, outs, args, scratch=(), flops=0):
    shapes = [jax.ShapeDtypeStruct(s, F32) for s in outs]
    size = sum(a.size * a.dtype.itemsize for a in args) + 4 * sum(int(np.prod(s)) for s in outs)
    vmem = pl.BlockSpec(memory_space=pltpu.VMEM)
    return pl.pallas_call(
        kernel,
        out_shape=shapes,
        in_specs=[vmem] * len(args),
        out_specs=[vmem] * len(outs),
        scratch_shapes=[pltpu.VMEM(s, F32) for s in scratch],
        compiler_params=pltpu.CompilerParams(vmem_limit_bytes=60 << 20),
        cost_estimate=pl.CostEstimate(flops=flops, bytes_accessed=size, transcendentals=0),
    )(*args)


def row_carry(leaving, sums, rates, size, reverse):
    count = leaving.shape[0] // 2
    me = lax.axis_index("row")
    core = me % 2
    swap = [(k, k ^ 1) for k in range(size)]
    other_sums = lax.ppermute(sums, "row", swap)
    mine = lax.dynamic_slice_in_dim(leaving, core * count, count, 0)
    theirs = lax.ppermute(
        lax.dynamic_slice_in_dim(leaving, (1 - core) * count, count, 0), "row", swap
    )
    rate = lax.dynamic_slice_in_dim(rates, core * count, count, 0)
    first = core == (1 if reverse else 0)
    near = jnp.where(first, mine, theirs)
    far = jnp.where(first, theirs, mine)
    near_sum = jnp.where(first, sums, other_sums)
    far_sum = jnp.where(first, other_sums, sums)
    total = far + jnp.exp2(rate * far_sum) * near
    sign = -2 if reverse else 2

    def shift(x, by):
        return lax.ppermute(
            x, "row", [(k, k + by) for k in range(size) if 0 <= k + by < size]
        )

    entering = shift(total, sign)
    if size > 4:
        span = shift(near_sum + far_sum, sign)
        by = sign
        while abs(by) < size - 2:
            entering = entering + jnp.exp2(rate * span) * shift(entering, by)
            span = span + shift(span, by)
            by *= 2
    to_far = near + jnp.exp2(rate * near_sum) * entering
    keep = jnp.where(first, entering, to_far)
    give = jnp.where(first, to_far, entering)
    got = lax.ppermute(give, "row", swap)
    return jnp.concatenate(
        [jnp.where(core == 0, keep, got), jnp.where(core == 0, got, keep)], 0
    )


def col_carry(leaving, sums, rates, size, reverse):
    states, rows, _ = leaving.shape
    share = rows // size
    me = lax.axis_index("col")
    send = jnp.concatenate([leaving, sums[None]], 0)
    send = send.reshape(states + 1, size, share, LANES).swapaxes(0, 1)
    held = lax.all_to_all(send, "col", 0, 0)
    rate = lax.dynamic_slice_in_dim(rates, me * share, share, 1)
    before = jnp.zeros((states, share, LANES), F32)
    parts = [None] * size
    for k in reversed(range(size)) if reverse else range(size):
        parts[k] = before
        before = jnp.exp2(rate * held[k, states]) * before + held[k, :states]
    back = lax.all_to_all(jnp.stack(parts), "col", 0, 0)
    return back.swapaxes(0, 1).reshape(states, rows, LANES)


def shards(features, step_size, write_weights, read_weights, decay_log, out_grad, sizes):
    rows, cols = sizes
    states = decay_log.shape[0]
    tile_h, tile_w = features.shape[:2]
    mats = lane_matrices()
    rate = -jnp.exp(decay_log) * LOG2E
    rates = jnp.broadcast_to(rate[:, :, None], (states, D, LANES))
    rates_v = jnp.repeat(rate.reshape(states, 2, 64).swapaxes(1, 2), 64, 2)
    rates_s = jnp.repeat(rate.reshape(states, 4, 32).swapaxes(1, 2), 32, 2)
    plane = (POS, D, LANES)
    seg = (states, 4, D, LANES)
    (step_p, source_p, write_p, cum_rows, cum_cols, sum_rows, sum_cols, seg_rows, leave_rows) = run(
        forward_rows_kernel,
        [plane, plane, (POS, states, LANES), plane, plane, (64, LANES), (32, LANES), seg,
         (states, 64, LANES)],
        [step_size, features, write_weights, rates, rates_v, mats["above"], mats["left"],
         mats["rows_out"], mats["cols_out"]],
    )
    enter_rows = row_carry(leave_rows, sum_rows, rates_v, rows, False)
    grad_p, read_p, seg_cols, leave_cols = run(
        adjoint_cols_kernel,
        [plane, (POS, states, LANES), seg, (states, 32, LANES)],
        [out_grad, read_weights, rates, cum_cols, mats["cols_out"]],
    )
    enter_cols = col_carry(leave_cols, sum_cols, rates_s, cols, True)
    start_rows, seg_s, leave_s = run(
        forward_cols_kernel,
        [seg, seg, (states, 32, LANES)],
        [seg_rows, enter_rows, step_p, source_p, write_p, rates, rates_s, cum_rows, cum_cols,
         sum_cols, mats["above"], mats["rows_in"], mats["cols_out"]],
    )
    enter_s = col_carry(leave_s, sum_cols, rates_s, cols, False)
    start_cols, seg_v, leave_v = run(
        adjoint_rows_kernel,
        [seg, seg, (states, 64, LANES)],
        [seg_cols, enter_cols, step_p, grad_p, read_p, rates, rates_s, cum_rows, cum_cols,
         sum_cols, mats["right"], mats["cols_in"], mats["rows_out"]],
    )
    enter_v = row_carry(leave_v, sum_rows, rates_v, rows, True)
    grad_features, grad_step, grad_write, grad_read, grad_decay = run(
        final_kernel,
        [features.shape, features.shape, (POS, states, LANES), (POS, states, LANES), (states, D)],
        [start_rows, start_cols, seg_s, enter_s, seg_v, enter_v, step_p, source_p, grad_p,
         write_p, read_p, rates, rates_v, cum_rows, cum_cols, sum_rows, mats["left"],
         mats["below"], mats["rows_in"], mats["cols_in"]],
        [seg, seg, (states, 64, LANES), plane, plane, (POS, states, 8, LANES),
         (POS, states, 8, LANES), (states, D, LANES)],
    )

    def unpack(x):
        x = x.reshape(BI, BJ, states, HS, WS).transpose(3, 0, 4, 1, 2)
        return x.reshape(tile_h, tile_w, states)

    return (
        grad_features,
        grad_step,
        unpack(grad_write),
        unpack(grad_read),
        lax.psum(grad_decay, ("row", "col")),
    )


def solution(mesh):
    spec = P("row", "col", None)
    sizes = (mesh.shape["row"], mesh.shape["col"])
    return jax.shard_map(
        functools.partial(shards, sizes=sizes),
        mesh=mesh,
        in_specs=(spec, spec, spec, spec, P(), spec),
        out_specs=(spec, spec, spec, spec, P()),
        check_vma=False,
    )
```

```python
import functools

import jax
import jax.numpy as jnp
import numpy as np
from jax import lax
from jax.experimental import pallas as pl
from jax.experimental.pallas import tpu as pltpu
from jax.sharding import PartitionSpec as P

HS, WS, BI, BJ = 8, 16, 4, 4
POS = BI * BJ
LANES = 128
D = 128
GROUPS = 1
CHANNELS = D // GROUPS
PACKS = 4
PACK = CHANNELS // PACKS
STEPS = 4
BLOCK = CHANNELS // STEPS
INNER = PACKS // STEPS
F32 = jnp.float32
BF16 = jnp.bfloat16
LOG2E = 1.4426950408889634
LN2 = 0.6931471805599453


@functools.cache
def lane_matrices():
    lane = np.arange(LANES)
    hs, ws = lane // WS, lane % WS
    same_w = ws[:, None] == ws[None]
    same_h = hs[:, None] == hs[None]
    above = same_w & (hs[:, None] < hs[None])
    below = same_w & (hs[:, None] > hs[None])
    left = same_h & (ws[:, None] < ws[None])
    right = same_h & (ws[:, None] > ws[None])
    rows_out = np.stack([
        np.stack([((b // 2) * 64 + j * WS + ws)[:, None] == lane[None] for j in range(BJ)])
        for b in range(PACKS)
    ])
    cols_out = np.stack([
        np.stack([(b * 32 + i * HS + hs)[:, None] == lane[None] for i in range(BI)])
        for b in range(PACKS)
    ])

    def twice(m):
        return np.concatenate([m, m], -2)

    def wide(m):
        return twice(np.concatenate([np.swapaxes(m[:, k], -1, -2) for k in range(m.shape[1])], -1))

    def beside(m, order):
        return twice(np.concatenate([m, np.broadcast_to(order, m.shape)], -1))

    out = {
        "above": twice(above), "left": twice(left),
        "rows_above": beside(rows_out, above), "rows_below": beside(rows_out, below),
        "cols_left": beside(cols_out, left), "cols_right": beside(cols_out, right),
        "rows_in": wide(rows_out), "cols_in": wide(cols_out),
    }
    return {k: v.astype(np.float32) for k, v in out.items()}


def halves(x):
    high = x.astype(BF16)
    low = (x - high.astype(F32)).astype(BF16)
    return high, low


def lane_dot(matrix, *parts):
    parts = [h for x in parts for h in halves(x)]
    return jnp.dot(jnp.concatenate(parts, 1), matrix, preferred_element_type=F32)


def lane_dot_exact(x, matrix):
    high, low = halves(x)
    rest = (x - high.astype(F32) - low.astype(F32)).astype(BF16)
    return jnp.dot(
        jnp.concatenate([high, low], 1), matrix, preferred_element_type=F32
    ) + jnp.dot(rest, matrix[:LANES], preferred_element_type=F32)


def row_of(ref, p, n):
    return jnp.broadcast_to(ref[p, pl.ds(n, 1), :], (8, LANES))


def each_group(states, size, body):
    groups = states // size

    def one(at, carry):
        d = pl.ds(pl.multiple_of((at // groups) * 8, 8), 8)
        body([(at % groups) * size + k for k in range(size)], d)
        return carry

    lax.fori_loop(0, (BLOCK // 8) * groups, one, 0)


def run_segments(seg, matrix, t):
    states = seg.shape[0]
    at = pl.ds(t * PACK, PACK)
    total = None
    for k in range(4):
        both = lane_dot(matrix[t, k], seg[:, k, at].reshape(states * PACK, LANES))
        seg[:, k, at] = both[:, LANES:].reshape(states, PACK, LANES)
        total = both[:, :LANES] if total is None else total + both[:, :LANES]
    return total.reshape(states, PACK, LANES)


def send(b, seg, matrix, leaving, rows):
    @pl.when(b == 0)
    def _():
        leaving[...] = jnp.zeros_like(leaving)

    for t in range(INNER):
        q = b * INNER + t
        at = pl.ds(pl.multiple_of((q % 2) * PACK, PACK), PACK) if rows else slice(None)
        leaving[:, at] += run_segments(seg, matrix, t)


def take(b, seg, entering, enter, out, rows):
    states = seg.shape[0]
    for t in range(INNER):
        q = b * INNER + t
        at = pl.ds(pl.multiple_of((q % 2) * PACK, PACK), PACK) if rows else slice(None)
        first = lane_dot(enter[t], entering[:, at].reshape(states * PACK, LANES))
        at = pl.ds(t * PACK, PACK)
        for k in range(4):
            out[:, k, at] = seg[:, k, at] + first[:, k * LANES : (k + 1) * LANES].reshape(
                states, PACK, LANES
            )


def gather_plane(ref, j):
    return jnp.concatenate([ref[hs, 0, pl.ds(j, WS, stride=BJ), :] for hs in range(HS)], 0).T


def gather_states(ref, turned, out):
    for hs in range(HS):
        turned[hs] = ref[hs, 0].T
    for j in range(BJ):
        out[j] = jnp.concatenate(
            [turned[hs, pl.ds(j, WS, stride=BJ), :] for hs in range(HS)], 0
        ).T


def pack_rates(decay_log, rates, rates_v, rates_s):
    lane = lax.broadcasted_iota(jnp.int32, (PACK, LANES), 1)
    lane_v = lax.broadcasted_iota(jnp.int32, (2 * PACK, LANES), 1)
    rate = (-LOG2E * jnp.exp(decay_log[0])).T
    for n in range(rates.shape[0]):
        r = jnp.broadcast_to(rate[:, n : n + 1], (D, LANES))
        rates[n] = r
        for g in range(GROUPS):
            part = [r[g * CHANNELS + k * PACK : g * CHANNELS + (k + 1) * PACK] for k in range(4)]
            rates_v[g, n] = jnp.where(
                lane_v < 64, jnp.concatenate(part[:2], 0), jnp.concatenate(part[2:], 0)
            )
            rates_s[g, n] = jnp.where(
                lane < 64, jnp.where(lane < 32, part[0], part[1]),
                jnp.where(lane < 96, part[2], part[3]),
            )


def adjoint_cols_kernel(
    step, grad, read, decay_log, left, cols_right,
    step_p, grad_p, read_p, rates, rates_v, rates_s, before_cols, sum_cols, seg, sent,
    all_step, all_grad, all_rates, turned, leaving, *, share,
):
    states = seg.shape[0]
    i = pl.program_id(0)
    b = i - BI

    @pl.when(i < BI)
    def _():
        for j in range(BJ):
            s, g = gather_plane(step, j), gather_plane(grad, j)
            step_p[j] = s
            grad_p[j] = g
            all_step[i * BJ + j] = s
            all_grad[i * BJ + j] = g
        at = pl.ds(i * BJ, BJ)
        gather_states(read, turned, read_p.at[at])
        pack_rates(decay_log, rates, rates_v, rates_s)
        all_rates[pl.ds(i * (states // BI), states // BI)] = rates[...]
        row_total = step_p[0]
        for j in range(1, BJ):
            row_total = row_total + step_p[j]
        before_cols[i] = lane_dot_exact(row_total, left[...])

        @pl.when(i == 0)
        def _():
            sum_cols[...] = jnp.zeros_like(sum_cols)

        for g in range(GROUPS):
            for q in range(PACKS):
                at = g * CHANNELS + q * PACK
                sum_cols[g] += lane_dot_exact(
                    row_total[at : at + PACK], cols_right[q, i, :, :LANES]
                )

    @pl.when(i >= BI)
    def _():
        def group(ns, d):
            wide = pl.ds(pl.multiple_of(b * BLOCK + d.start, 8), 8)
            r = [all_rates[n, wide] for n in ns]
            for i in range(BI):
                acc = [None] * len(ns)
                c = before_cols[i, wide]
                for j in range(BJ):
                    p = i * BJ + j
                    c = c + all_step[p, wide]
                    g = all_grad[p, wide]
                    for k, n in enumerate(ns):
                        term = jnp.exp2(c * r[k]) * g * row_of(read_p, p, n)
                        acc[k] = term if acc[k] is None else acc[k] + term
                for k, n in enumerate(ns):
                    seg[n, i, d] = acc[k]

        each_group(states, 8, group)
        send(b, seg, cols_right.at[pl.ds(b * INNER, INNER)], leaving, False)

        @pl.when(b == STEPS - 1)
        def _():
            for k in range(states // share):
                sent[k, 0:share] = leaving[k * share : (k + 1) * share]
                sent[k, share] = sum_cols[0]


def forward_rows_kernel(
    feat, write, step_p, rates, rates_v, above, rows_above,
    source_p, write_p, before_rows, sum_rows, seg, leaving,
    all_step, all_source, turned, col_total,
):
    states = seg.shape[0]
    i = pl.program_id(0)
    b = i - BI

    @pl.when(i < BI)
    def _():
        for j in range(BJ):
            s = step_p[j]
            f = s * gather_plane(feat, j)
            source_p[j] = f
            all_step[i * BJ + j] = s
            all_source[i * BJ + j] = f
        gather_states(write, turned, write_p.at[pl.ds(i * BJ, BJ)])

        @pl.when(i == 0)
        def _():
            col_total[...] = step_p[...]

        @pl.when(i > 0)
        def _():
            col_total[...] += step_p[...]

        @pl.when(i == BI - 1)
        def _():
            for j in range(BJ):
                before_rows[j] = lane_dot_exact(col_total[j], above[...])
            for g in range(GROUPS):
                for r in range(2):
                    total = None
                    for q in (r, r + 2):
                        at = g * CHANNELS + q * PACK
                        for j in range(BJ):
                            one = lane_dot_exact(
                                col_total[j, at : at + PACK], rows_above[q, j, :, :LANES]
                            )
                            total = one if total is None else total + one
                    sum_rows[g, r * PACK : (r + 1) * PACK] = total

    @pl.when(i >= BI)
    def _():
        def group(ns, d):
            wide = pl.ds(pl.multiple_of(b * BLOCK + d.start, 8), 8)
            r = [-rates[n, d] for n in ns]
            for j in range(BJ):
                acc = [None] * len(ns)
                c = before_rows[j, wide]
                for i in range(BI):
                    p = i * BJ + j
                    c = c + all_step[p, wide]
                    s = all_source[p, wide]
                    for k, n in enumerate(ns):
                        term = jnp.exp2(c * r[k]) * s * row_of(write_p, p, n)
                        acc[k] = term if acc[k] is None else acc[k] + term
                for k, n in enumerate(ns):
                    seg[n, j, d] = acc[k]

        each_group(states, 8, group)
        send(b, seg, rows_above.at[pl.ds(b * INNER, INNER)], leaving, True)

        @pl.when(b == STEPS - 1)
        def _():
            for n in range(states):
                leaving[n] = leaving[n] * jnp.exp2(rates_v[0, n] * sum_rows[0])


def forward_cols_kernel(
    seg_rows, entering, step_p, source_p, write_p, rates, rates_s, before_rows, before_cols,
    sum_cols, rows_in, cols_out, start_rows, seg, leaving,
):
    states = seg.shape[0]
    b = pl.program_id(0)
    take(b, seg_rows, entering, rows_in, start_rows, True)

    def group(ns, d):
        r = [rates[n, d] for n in ns]
        vert = [[None] * BJ for _ in ns]
        for j in range(BJ):
            before = before_rows[j, d]
            for k, n in enumerate(ns):
                vert[k][j] = start_rows[n, j, d] * jnp.exp2(r[k] * before)
                start_rows[n, j, d] = vert[k][j]
        for i in range(BI):
            state = [None] * len(ns)
            after = before_cols[i, d]
            for j in range(BJ):
                p = i * BJ + j
                c, s = step_p[p, d], source_p[p, d]
                after = after + c
                for k, n in enumerate(ns):
                    decay = jnp.exp2(c * r[k])
                    vert[k][j] = decay * vert[k][j] + s * row_of(write_p, p, n)
                    state[k] = vert[k][j] if j == 0 else decay * state[k] + vert[k][j]
            for k, n in enumerate(ns):
                seg[n, i, d] = state[k] * jnp.exp2(-r[k] * after)

    each_group(states, 8, group)
    send(b, seg, cols_out, leaving, False)

    @pl.when(b == STEPS - 1)
    def _():
        for n in range(states):
            leaving[n] = leaving[n] * jnp.exp2(rates_s[0, n] * sum_cols[0])


def adjoint_rows_kernel(
    seg_cols, entering, step_p, grad_p, read_p, rates, rates_s, before_rows, before_cols,
    sum_cols, cols_in, rows_out, start_cols, seg, leaving, scaled,
):
    states = seg.shape[0]
    b = pl.program_id(0)

    @pl.when(b == 0)
    def _():
        for n in range(states):
            scaled[n] = entering[n] * jnp.exp2(rates_s[0, n] * sum_cols[0])

    take(b, seg_cols, scaled, cols_in, start_cols, False)

    def group(ns, d):
        r = [rates[n, d] for n in ns]
        passed_v = [[None] * BJ for _ in ns]
        for i in reversed(range(BI)):
            after = before_cols[i, d]
            for j in range(BJ):
                after = after + step_p[i * BJ + j, d]
            passed = []
            for k, n in enumerate(ns):
                passed.append(start_cols[n, i, d] * jnp.exp2(-r[k] * after))
                start_cols[n, i, d] = passed[k]
            for j in reversed(range(BJ)):
                p = i * BJ + j
                c, g = step_p[p, d], grad_p[p, d]
                for k, n in enumerate(ns):
                    decay = jnp.exp2(c * r[k])
                    adjoint = g * row_of(read_p, p, n) + passed[k]
                    passed[k] = decay * adjoint
                    if i == BI - 1:
                        passed_v[k][j] = passed[k]
                    else:
                        passed_v[k][j] = decay * (adjoint + passed_v[k][j])
        for j in range(BJ):
            before = before_rows[j, d]
            for k, n in enumerate(ns):
                seg[n, j, d] = passed_v[k][j] * jnp.exp2(r[k] * before)

    each_group(states, 8, group)
    send(b, seg, rows_out, leaving, True)


def final_kernel(
    start_rows, start_cols, seg_s, enter_s, seg_v, enter_v,
    step_p, source_p, grad_p, write_p, read_p, rates, rates_v, before_rows, before_cols, sum_rows,
    cols_in, rows_in,
    features_p, steps_p, sum_w, sum_r, grad_decay,
    in_s, in_v, scaled_v, decay_term, through, rate_term,
):
    states = rates.shape[0]
    b = pl.program_id(0)

    @pl.when(b == 0)
    def _():
        for n in range(states):
            scaled_v[n] = enter_v[n] * jnp.exp2(rates_v[0, n] * sum_rows[0])
        sum_w[...] = jnp.zeros_like(sum_w)
        sum_r[...] = jnp.zeros_like(sum_r)

    take(b, seg_s, enter_s, cols_in, in_s, False)
    take(b, seg_v, scaled_v, rows_in, in_v, True)
    through[...] = jnp.zeros_like(through)
    rate_term[...] = jnp.zeros_like(rate_term)

    def group(ns, d):
        many = range(len(ns))
        r = [rates[n, d] for n in ns]
        vert = [[start_rows[n, j, d] for j in range(BJ)] for n in ns]
        from_v, from_s = [{} for _ in many], [{} for _ in many]
        for i in range(BI):
            before = before_cols[i, d]
            state = [in_s[n, i, d] * jnp.exp2(r[k] * before) for k, n in enumerate(ns)]
            for j in range(BJ):
                p = i * BJ + j
                c, s, g = step_p[p, d], source_p[p, d], grad_p[p, d]
                for k, n in enumerate(ns):
                    m = c * r[k]
                    decay = jnp.exp2(m)
                    dv = decay * vert[k][j]
                    vert[k][j] = dv + s * row_of(write_p, p, n)
                    ds = decay * state[k]
                    state[k] = ds + vert[k][j]
                    sum_r[p, pl.ds(n * 8, 8)] += state[k] * g
                    from_v[k][p] = dv
                    from_s[k][p] = ds
        passed_v = [[None] * BJ for _ in ns]
        for j in range(BJ):
            after = before_rows[j, d]
            for i in range(BI):
                after = after + step_p[i * BJ + j, d]
            for k, n in enumerate(ns):
                passed_v[k][j] = in_v[n, j, d] * jnp.exp2(-r[k] * after)
        total = [None for _ in ns]
        for i in reversed(range(BI)):
            passed = [start_cols[n, i, d] for n in ns]
            for j in reversed(range(BJ)):
                p = i * BJ + j
                c, s, g = step_p[p, d], source_p[p, d], grad_p[p, d]
                sum_q, sum_t = None, None
                for k, n in enumerate(ns):
                    adjoint = g * row_of(read_p, p, n) + passed[k]
                    m = c * r[k]
                    decay = jnp.exp2(m)
                    passed[k] = decay * adjoint
                    adjoint_v = adjoint + passed_v[k][j]
                    passed_v[k][j] = decay * adjoint_v
                    q = (adjoint * from_s[k][p] + adjoint_v * from_v[k][p]) * m
                    total[k] = q if total[k] is None else total[k] + q
                    t = adjoint_v * row_of(write_p, p, n)
                    sum_q = q if sum_q is None else sum_q + q
                    sum_t = t if sum_t is None else sum_t + t
                    sum_w[p, pl.ds(n * 8, 8)] += adjoint_v * s
                rate_term[p, d] += sum_q
                through[p, d] += sum_t
        for k, n in enumerate(ns):
            decay_term[n, d] = total[k]

    each_group(states, 8, group)
    for p in range(POS):
        t = through[p]
        s = step_p[p]
        features_p[p] = s * t
        steps_p[p] = (source_p[p] * t + rate_term[p] * LN2) / s
    for n in range(states):
        all_decay = lax.dot_general(
            jnp.ones((8, 2 * LANES), BF16), jnp.concatenate(halves(decay_term[n]), 1),
            (((1,), (1,)), ((), ())), preferred_element_type=F32,
        )
        grad_decay[0, pl.ds(n, 1)] = all_decay[0:1] * LN2


def unpack_kernel(features_p, steps_p, sum_w, sum_r, features, steps, writes, reads, turned):
    for j in range(BJ):
        for values, out in ((features_p, features), (steps_p, steps)):
            back = values[j].T
            for hs in range(HS):
                out[hs, 0, pl.ds(j, WS, stride=BJ), :] = back[hs * WS : hs * WS + WS]
    for values, out in ((sum_w, writes), (sum_r, reads)):
        for j in range(BJ):
            states = writes.shape[2]
            back = sum(values[j, pl.ds(k, states, stride=8), :] for k in range(8)).T
            for hs in range(HS):
                turned[hs, pl.ds(j, WS, stride=BJ), :] = back[hs * WS : hs * WS + WS]
        for hs in range(HS):
            out[hs, 0] = turned[hs].T


def prefix_kernel(held, sums, rates, out, *, reverse):
    size, share = out.shape[:2]
    at = sums.shape[1] - 1
    order = list(reversed(range(size))) if reverse else list(range(size))
    for n in range(share):
        before = jnp.zeros(out.shape[2:], F32)
        for k in order:
            out[k, n] = before
            before = jnp.exp2(rates[n] * sums[k, at]) * before + held[k, n]


def run(kernel, ins, outs, scratch=(), group=0, micros=5, steps=STEPS, lead=0, limit=60):
    parts = lead if lead else steps

    def early(b):
        return jnp.minimum(b, lead - 1) if lead else b

    def late(b):
        return jnp.maximum(b - lead, 0) if lead else b

    def spec(shape, kind):
        rank = len(shape)
        block, at = list(shape), [None] * rank
        if kind == "first":
            block[0], at[0] = shape[0] // parts, early
        elif kind == "second":
            block[1], at[1] = 1, early
        elif kind == "states":
            block[1], at[1] = shape[1] // parts, early
        elif kind == "group":
            block[0], at[0] = 1, lambda b: group
        elif kind == "plane":
            block[-2], at[-2] = BLOCK, lambda b: group * STEPS + late(b)
        elif kind == "own":
            block[-2], at[-2] = BLOCK, late
        return pl.BlockSpec(tuple(block), lambda b: tuple(0 if f is None else f(b) for f in at))

    return pl.pallas_call(
        kernel,
        grid=(lead + steps,),
        out_shape=[jax.ShapeDtypeStruct(s, F32) for s, _ in outs],
        in_specs=[spec(a.shape, kind) for a, kind in ins],
        out_specs=[spec(s, kind) for s, kind in outs],
        scratch_shapes=[pltpu.VMEM(s, F32) for s in scratch],
        compiler_params=pltpu.CompilerParams(
            vmem_limit_bytes=limit << 20, dimension_semantics=("arbitrary",)
        ),
        cost_estimate=pl.CostEstimate(
            flops=0, bytes_accessed=int(micros * 3.3e6), transcendentals=0
        ),
    )(*[a for a, _ in ins])


def swap_cores(x, size):
    return lax.ppermute(x, "row", [(k, k ^ 1) for k in range(size)])


def tied(*arrays):
    return lax.optimization_barrier(arrays)


def row_total(leaving, sums, other_sums, rates, size, reverse):
    count = leaving.shape[0] // 2
    core = lax.axis_index("row") % 2
    mine = lax.dynamic_slice_in_dim(leaving, core * count, count, 0)
    theirs = swap_cores(lax.dynamic_slice_in_dim(leaving, (1 - core) * count, count, 0), size)
    rate = lax.dynamic_slice_in_dim(rates, core * count, count, 0)
    first = core == (1 if reverse else 0)
    near = jnp.where(first, mine, theirs)
    far = jnp.where(first, theirs, mine)
    near_sum = jnp.where(first, sums, other_sums)
    far_sum = jnp.where(first, other_sums, sums)
    total = far + jnp.exp2(rate * far_sum) * near
    return total, near, near_sum, far_sum, rate


def row_carry(total, near, near_sum, far_sum, rate, beside, size, reverse):
    core = lax.axis_index("row") % 2
    first = core == (1 if reverse else 0)
    sign = -2 if reverse else 2

    def shift(x, by):
        return lax.ppermute(
            x, "row", [(k, k + by) for k in range(size) if 0 <= k + by < size]
        )

    entering = shift(total, sign)
    if size > 4:
        span = shift(near_sum + far_sum, sign)
        by = sign
        while abs(by) < size - 2:
            entering = entering + jnp.exp2(rate * span) * shift(entering, by)
            span = span + shift(span, by)
            by *= 2
    entering, _ = tied(entering, beside)
    to_far = near + jnp.exp2(rate * near_sum) * entering
    keep = jnp.where(first, entering, to_far)
    got = swap_cores(jnp.where(first, to_far, entering), size)
    return jnp.concatenate(
        [jnp.where(core == 0, keep, got), jnp.where(core == 0, got, keep)], 0
    )


def col_gather(sent):
    return lax.all_to_all(sent, "col", 0, 0)


def col_carry(held, sums, rates, reverse):
    size, share = held.shape[0], rates.shape[0]
    vmem = pl.BlockSpec(memory_space=pltpu.VMEM)
    return pl.pallas_call(
        functools.partial(prefix_kernel, reverse=reverse),
        out_shape=jax.ShapeDtypeStruct((size, share) + held.shape[2:], F32),
        in_specs=[vmem] * 3,
        out_specs=vmem,
        compiler_params=pltpu.CompilerParams(vmem_limit_bytes=4 << 20),
    )(held, sums, rates)


def col_return(carries):
    back = lax.all_to_all(carries, "col", 0, 0)
    return back.reshape((-1,) + carries.shape[2:])


def total_of(x, rows, cols):
    for axis, size in (("row", rows), ("col", cols)):
        by = 1
        while by < size:
            x = x + lax.ppermute(x, axis, [(k, k ^ by) for k in range(size)])
            by *= 2
    return x


def shards(features, step_size, write_weights, read_weights, decay_log, out_grad, sizes):
    rows, cols = sizes
    states = decay_log.shape[0]
    share = states // cols
    tile_h, tile_w = features.shape[:2]
    mats = {k: jnp.asarray(v, BF16) for k, v in lane_matrices().items()}
    plane, quad = (POS, D, LANES), (4, D, LANES)
    seg = (states, 4, CHANNELS, LANES)
    small = (POS, states, LANES)
    packed = (HS, BI, tile_w, D)
    weights = (HS, BI, states, tile_w)
    size_v, size_s = (states, CHANNELS // 2, LANES), (states, CHANNELS // 4, LANES)
    me = lax.axis_index("col")
    todo = range(GROUPS)
    enter_rows, enter_cols, enter_s, enter_v = {}, {}, {}, {}
    seg_rows, seg_cols, seg_s, seg_v, start_rows, start_cols, col_sums = {}, {}, {}, {}, {}, {}, {}
    rate_s = {}
    for g in todo:
        (step_p, grad_p, read_p, rates, rates_v, rates_s, before_cols, sum_cols, seg_cols[g],
         sent) = run(
            functools.partial(adjoint_cols_kernel, share=share),
            [(step_size.reshape(packed), "second"), (out_grad.reshape(packed), "second"),
             (read_weights.swapaxes(1, 2).reshape(weights), "second"),
             (decay_log.reshape(BI, states // BI, D), "first"), (mats["left"], "whole"),
             (mats["cols_right"], "whole")],
            [(plane, "first"), (plane, "first"), (small, "whole"),
             ((states, D, LANES), "first"), ((GROUPS,) + size_v, "states"),
             ((GROUPS,) + size_s, "states"), (quad, "whole"), ((GROUPS,) + size_s[1:], "whole"),
             (seg, "own"), ((cols, share + 1) + size_s[1:], "whole")],
            [plane, plane, (states, D, LANES), (HS, tile_w, states), size_s], g, lead=BI,
        )
        rate_s[g] = lax.dynamic_slice_in_dim(rates_s[g], me * share, share, 0)
        held = col_gather(sent)
        step_p, _, rate_s[g] = tied(step_p, sent, rate_s[g])
        source_p, write_p, before_rows, sum_rows, seg_rows[g], leave_rows = run(
            forward_rows_kernel,
            [(features.reshape(packed), "second"),
             (write_weights.swapaxes(1, 2).reshape(weights), "second"), (step_p, "first"),
             (rates, "plane"), (rates_v, "group"), (mats["above"], "whole"),
             (mats["rows_above"], "whole")],
            [(plane, "first"), (small, "whole"), (quad, "whole"),
             ((GROUPS,) + size_v[1:], "whole"), (seg, "own"), (size_v, "whole")],
            [plane, plane, (HS, tile_w, states), quad], g, lead=BI,
        )
        other_rows = swap_cores(sum_rows, rows)
        total = row_total(leave_rows, sum_rows[g], other_rows[g], rates_v[g], rows, False)
        held, first = tied(held, total[0])
        col_sums[g] = held
        carries = col_carry(held, held, rate_s[g], True)
        enter_cols[g] = col_return(carries)
        enter_rows[g] = row_carry(first, *total[1:], carries, rows, False)
    for g in todo:
        start_rows[g], seg_s[g], leave_s = run(
            forward_cols_kernel,
            [(seg_rows[g], "own"), (enter_rows[g], "whole"), (step_p, "plane"),
             (source_p, "plane"), (write_p, "whole"), (rates, "plane"), (rates_s, "group"),
             (before_rows, "plane"), (before_cols, "plane"), (sum_cols, "group"),
             (mats["rows_in"], "first"), (mats["cols_left"], "first")],
            [(seg, "own"), (seg, "own"), (size_s, "whole")], (), g, 10,
        )
        held = col_gather(leave_s.reshape((cols, share) + size_s[1:]))
        enter_cols[g], _ = tied(enter_cols[g], leave_s)
        start_cols[g], seg_v[g], leave_v = run(
            adjoint_rows_kernel,
            [(seg_cols[g], "own"), (enter_cols[g], "whole"), (step_p, "plane"),
             (grad_p, "plane"), (read_p, "whole"), (rates, "plane"), (rates_s, "group"),
             (before_rows, "plane"), (before_cols, "plane"), (sum_cols, "group"),
             (mats["cols_in"], "first"), (mats["rows_below"], "first")],
            [(seg, "own"), (seg, "own"), (size_v, "whole")], [size_s], g, 10,
        )
        held, leave_v = tied(held, leave_v)
        carries = col_carry(held, col_sums[g], rate_s[g], False)
        enter_s[g] = col_return(carries)
        leave_v, carries = tied(leave_v, carries)
        total = row_total(leave_v, sum_rows[g], other_rows[g], rates_v[g], rows, True)
        enter_v[g] = row_carry(*total, enter_s[g], rows, True)
    sums = (POS, states * 8, LANES)
    own_plane = (POS, CHANNELS, LANES)
    parts = []
    for g in todo:
        parts.append(run(
            final_kernel,
            [(start_rows[g], "own"), (start_cols[g], "own"), (seg_s[g], "own"),
             (enter_s[g], "whole"), (seg_v[g], "own"), (enter_v[g], "whole"), (step_p, "plane"),
             (source_p, "plane"), (grad_p, "plane"), (write_p, "whole"), (read_p, "whole"),
             (rates, "plane"), (rates_v, "group"), (before_rows, "plane"),
             (before_cols, "plane"), (sum_rows, "group"), (mats["cols_in"], "first"), (mats["rows_in"], "first")],
            [(own_plane, "own"), (own_plane, "own"), (sums, "whole"), (sums, "whole"),
             ((STEPS, states, BLOCK), "first")],
            [(states, 4, BLOCK, LANES), (states, 4, BLOCK, LANES), size_v,
             (states, BLOCK, LANES), (POS, BLOCK, LANES), (POS, BLOCK, LANES)],
            g, 27,
        ))
    features_p, steps_p, sum_w, sum_r, grad_decay = parts[0]
    grad_decay = grad_decay.swapaxes(0, 1).reshape(states, D)
    grad_decay = total_of(grad_decay, rows, cols)
    grad_features, grad_step, grad_write, grad_read = run(
        unpack_kernel,
        [(features_p, "first"), (steps_p, "first"), (sum_w, "first"), (sum_r, "first")],
        [(packed, "second"), (packed, "second"), (weights, "second"), (weights, "second")],
        [(HS, tile_w, states)], 0, 5, BI,
    )
    weights = (tile_h, states, tile_w)
    return (
        grad_features.reshape(features.shape),
        grad_step.reshape(features.shape),
        grad_write.reshape(weights).swapaxes(1, 2),
        grad_read.reshape(weights).swapaxes(1, 2),
        grad_decay,
    )


def solution(mesh):
    spec = P("row", "col", None)
    sizes = (mesh.shape["row"], mesh.shape["col"])
    return jax.shard_map(
        functools.partial(shards, sizes=sizes),
        mesh=mesh,
        in_specs=(spec, spec, spec, spec, P(), spec),
        out_specs=(spec, spec, spec, spec, P()),
        check_vma=False,
    )
```

```python
import functools

import jax
import jax.numpy as jnp
import numpy as np
from jax import lax
from jax.experimental import pallas as pl
from jax.experimental.pallas import tpu as pltpu
from jax.sharding import PartitionSpec as P

HS, WS, BI, BJ = 8, 16, 4, 4
POS = BI * BJ
LANES = 128
D = 128
STEPS = 4
BLOCK = D // STEPS
F32 = jnp.float32
BF16 = jnp.bfloat16
LOG2E = 1.4426950408889634
LN2 = 0.6931471805599453


@functools.cache
def lane_orders():
    lane = np.arange(LANES)
    hs, ws = lane // WS, lane % WS
    same_w = ws[:, None] == ws[None]
    same_h = hs[:, None] == hs[None]
    out = {
        "above": same_w & (hs[:, None] < hs[None]), "below": same_w & (hs[:, None] > hs[None]),
        "left": same_h & (ws[:, None] < ws[None]), "right": same_h & (ws[:, None] > ws[None]),
    }
    return {k: np.concatenate([v, v], 0).astype(np.float32) for k, v in out.items()}


def lane_places(rows, out):
    at = lax.broadcasted_iota(jnp.int32, (2 * LANES, LANES), 0) % LANES
    lane = lax.broadcasted_iota(jnp.int32, (2 * LANES, LANES), 1)
    segment, edge = (at, lane) if out else (lane, at)
    return edge - (segment % WS if rows else segment // WS)


def edge_start(b, k, rows):
    return (b // 2) * 64 + k * WS if rows else b * 32 + k * HS


def placed(places, start):
    return jnp.where(places == start, 1.0, 0.0).astype(BF16)


def halves(x):
    high = x.astype(BF16)
    low = (x - high.astype(F32)).astype(BF16)
    return high, low


def lane_dot(matrix, *parts):
    parts = [h for x in parts for h in halves(x)]
    return jnp.dot(jnp.concatenate(parts, 1), matrix, preferred_element_type=F32)


def lane_dot_exact(x, matrix):
    high, low = halves(x)
    rest = (x - high.astype(F32) - low.astype(F32)).astype(BF16)
    return jnp.dot(
        jnp.concatenate([high, low], 1), matrix, preferred_element_type=F32
    ) + jnp.dot(rest, matrix[:LANES], preferred_element_type=F32)


def row_of(ref, p, n):
    return jnp.broadcast_to(ref[p, pl.ds(n, 1), :], (8, LANES))


def block_of(b):
    return pl.ds(pl.multiple_of(b * BLOCK, BLOCK), BLOCK)


def half_of(b):
    return pl.ds(pl.multiple_of((b % 2) * BLOCK, BLOCK), BLOCK)


def each_group(b, states, size, body):
    groups = states // size

    def one(at, carry):
        d = pl.ds(pl.multiple_of(b * BLOCK + (at // groups) * 8, 8), 8)
        body([(at % groups) * size + k for k in range(size)], d)
        return carry

    lax.fori_loop(0, (BLOCK // 8) * groups, one, 0)


def send(b, seg, order, leaving, rows):
    states = seg.shape[0]
    at = block_of(b)
    total = None
    places = lane_places(rows, True)
    for k in range(4):
        matrix = jnp.concatenate([placed(places, edge_start(b, k, rows)), order[...]], 1)
        both = lane_dot(matrix, seg[:, k, at].reshape(states * BLOCK, LANES))
        seg[:, k, at] = both[:, LANES:].reshape(states, BLOCK, LANES)
        total = both[:, :LANES] if total is None else total + both[:, :LANES]
    total = total.reshape(states, BLOCK, LANES)
    if rows:
        leaving[:, half_of(b)] += total
    else:
        leaving[...] += total


def take(b, seg, entering, out, rows):
    states = seg.shape[0]
    entering = entering[:, half_of(b)] if rows else entering[...]
    places = lane_places(rows, False)
    matrix = jnp.concatenate([placed(places, edge_start(b, k, rows)) for k in range(4)], 1)
    first = lane_dot(matrix, entering.reshape(states * BLOCK, LANES))
    at = block_of(b)
    for k in range(4):
        out[:, k, at] = seg[:, k, at] + first[:, k * LANES : (k + 1) * LANES].reshape(
            states, BLOCK, LANES
        )


def part_by_core(core, whole, keep, give):
    count = whole.shape[0] // 2
    for n in range(count):
        low, high = whole[n], whole[count + n]
        keep[n] = jnp.where(core[0] == 0, low, high)
        give[n] = jnp.where(core[0] == 0, high, low)


def join_by_core(core, keep, got, whole):
    count = whole.shape[0] // 2
    for n in range(count):
        whole[n] = jnp.where(core[0] == 0, keep[n], got[n])
        whole[count + n] = jnp.where(core[0] == 0, got[n], keep[n])


def gather_plane(ref, i, j):
    return jnp.concatenate([ref[hs, i, pl.ds(j, WS, stride=BJ), :] for hs in range(HS)], 0).T


def gather_states(ref, i, turned, out):
    for hs in range(HS):
        turned[hs] = ref[hs, i].T
    for j in range(BJ):
        out[i * BJ + j] = jnp.concatenate(
            [turned[hs, pl.ds(j, WS, stride=BJ), :] for hs in range(HS)], 0
        ).T


def pack_rates(i, decay_log, rates, rates_v, rates_s):
    lane = lax.broadcasted_iota(jnp.int32, (BLOCK, LANES), 1)
    lane_v = lax.broadcasted_iota(jnp.int32, (2 * BLOCK, LANES), 1)
    rate = (-LOG2E * jnp.exp(decay_log[i])).T
    count = rates.shape[0] // BI
    for k in range(count):
        n = i * count + k
        r = jnp.broadcast_to(rate[:, k : k + 1], (D, LANES))
        rates[n] = r
        part = [r[q * BLOCK : (q + 1) * BLOCK] for q in range(4)]
        rates_v[n] = jnp.where(lane_v < 64, r[: 2 * BLOCK], r[2 * BLOCK :])
        rates_s[n] = jnp.where(
            lane < 64, jnp.where(lane < 32, part[0], part[1]),
            jnp.where(lane < 96, part[2], part[3]),
        )


class AdjointCols:
    def first(self, step, grad, read, decay_log, place, left, right,
              step_p, grad_p, rates, seg, read_p, rates_v, rates_s, own_rates, before_cols,
              sum_cols, sum_rows, sent, turned, leaving):
        sum_cols[...] = jnp.zeros_like(sum_cols)
        leaving[...] = jnp.zeros_like(leaving)

    def lead(self, i, step, grad, read, decay_log, place, left, right,
             step_p, grad_p, rates, seg, read_p, rates_v, rates_s, own_rates, before_cols,
             sum_cols, sum_rows, sent, turned, leaving):
        row_total = None
        for j in range(BJ):
            s = gather_plane(step, i, j)
            step_p[i * BJ + j] = s
            grad_p[i * BJ + j] = gather_plane(grad, i, j)
            row_total = s if row_total is None else row_total + s
        gather_states(read, i, turned, read_p)
        pack_rates(i, decay_log, rates, rates_v, rates_s)
        before_cols[i] = lane_dot_exact(row_total, left[...])
        places = lane_places(False, True)
        for q in range(STEPS):
            sum_cols[...] += lane_dot_exact(
                row_total[q * BLOCK : (q + 1) * BLOCK], placed(places, edge_start(q, i, False))
            )

    def main(self, b, step, grad, read, decay_log, place, left, right,
             step_p, grad_p, rates, seg, read_p, rates_v, rates_s, own_rates, before_cols,
             sum_cols, sum_rows, sent, turned, leaving):
        states = seg.shape[0]

        def group(ns, d):
            r = [rates[n, d] for n in ns]
            for i in range(BI):
                acc = [None] * len(ns)
                c = before_cols[i, d]
                for j in range(BJ):
                    p = i * BJ + j
                    c = c + step_p[p, d]
                    g = grad_p[p, d]
                    for k, n in enumerate(ns):
                        term = jnp.exp2(c * r[k]) * g * row_of(read_p, p, n)
                        acc[k] = term if acc[k] is None else acc[k] + term
                for k, n in enumerate(ns):
                    seg[n, i, d] = acc[k]

        each_group(b, states, 16, group)
        send(b, seg, right, leaving, False)

    def last(self, step, grad, read, decay_log, place, left, right,
             step_p, grad_p, rates, seg, read_p, rates_v, rates_s, own_rates, before_cols,
             sum_cols, sum_rows, sent, turned, leaving):
        share = own_rates.shape[0]
        for k in range(sent.shape[0]):
            sent[k, 0:share] = leaving[k * share : (k + 1) * share]
            sent[k, share] = sum_cols[...]
        for k in range(share):
            own_rates[k] = rates_s[place[0] * share + k]
        places = lane_places(True, True)
        for r in range(2):
            total = None
            for q in (r, r + 2):
                for j in range(BJ):
                    run = None
                    for i in range(BI):
                        s = step_p[i * BJ + j, q * BLOCK : (q + 1) * BLOCK]
                        run = s if run is None else run + s
                    one = lane_dot_exact(run, placed(places, edge_start(q, j, True)))
                    total = one if total is None else total + one
            sum_rows[r * BLOCK : (r + 1) * BLOCK] = total


class ForwardRows:
    def first(self, feat, step_p, rates, write, rates_v, sum_rows, core, above,
              source_p, seg, write_p, before_rows, keep, give, turned, leaving):
        leaving[...] = jnp.zeros_like(leaving)

    def lead(self, i, feat, step_p, rates, write, rates_v, sum_rows, core, above,
             source_p, seg, write_p, before_rows, keep, give, turned, leaving):
        for j in range(BJ):
            source_p[i * BJ + j] = step_p[i * BJ + j] * gather_plane(feat, i, j)
        gather_states(write, i, turned, write_p)

        @pl.when(i == BI - 1)
        def _():
            for j in range(BJ):
                run = step_p[j]
                for k in range(1, BI):
                    run = run + step_p[k * BJ + j]
                before_rows[j] = lane_dot_exact(run, above[...])

    def main(self, b, feat, step_p, rates, write, rates_v, sum_rows, core, above,
             source_p, seg, write_p, before_rows, keep, give, turned, leaving):
        states = seg.shape[0]

        def group(ns, d):
            r = [-rates[n, d] for n in ns]
            for j in range(BJ):
                acc = [None] * len(ns)
                c = before_rows[j, d]
                for i in range(BI):
                    p = i * BJ + j
                    c = c + step_p[p, d]
                    s = source_p[p, d]
                    for k, n in enumerate(ns):
                        term = jnp.exp2(c * r[k]) * s * row_of(write_p, p, n)
                        acc[k] = term if acc[k] is None else acc[k] + term
                for k, n in enumerate(ns):
                    seg[n, j, d] = acc[k]

        each_group(b, states, 16, group)
        send(b, seg, above, leaving, True)

    def last(self, feat, step_p, rates, write, rates_v, sum_rows, core, above,
             source_p, seg, write_p, before_rows, keep, give, turned, leaving):
        for n in range(leaving.shape[0]):
            leaving[n] = leaving[n] * jnp.exp2(rates_v[n] * sum_rows[...])
        part_by_core(core, leaving, keep, give)


class ForwardCols:
    def first(self, step_p, source_p, rates, seg_rows, keep, got, write_p, rates_s, before_rows,
              before_cols, sum_cols, core, left, start_rows, seg, leaving, entering):
        leaving[...] = jnp.zeros_like(leaving)
        join_by_core(core, keep, got, entering)

    def main(self, b, step_p, source_p, rates, seg_rows, keep, got, write_p, rates_s, before_rows,
             before_cols, sum_cols, core, left, start_rows, seg, leaving, entering):
        states = seg.shape[0]
        take(b, seg_rows, entering, start_rows, True)

        def group(ns, d):
            r = [rates[n, d] for n in ns]
            vert = [[None] * BJ for _ in ns]
            for j in range(BJ):
                before = before_rows[j, d]
                for k, n in enumerate(ns):
                    vert[k][j] = start_rows[n, j, d] * jnp.exp2(r[k] * before)
                    start_rows[n, j, d] = vert[k][j]
            for i in range(BI):
                state = [None] * len(ns)
                after = before_cols[i, d]
                for j in range(BJ):
                    p = i * BJ + j
                    c, s = step_p[p, d], source_p[p, d]
                    after = after + c
                    for k, n in enumerate(ns):
                        decay = jnp.exp2(c * r[k])
                        vert[k][j] = decay * vert[k][j] + s * row_of(write_p, p, n)
                        state[k] = vert[k][j] if j == 0 else decay * state[k] + vert[k][j]
                for k, n in enumerate(ns):
                    seg[n, i, d] = state[k] * jnp.exp2(-r[k] * after)

        each_group(b, states, 8, group)
        send(b, seg, left, leaving, False)

    def last(self, step_p, source_p, rates, seg_rows, keep, got, write_p, rates_s, before_rows,
             before_cols, sum_cols, core, left, start_rows, seg, leaving, entering):
        for n in range(leaving.shape[0]):
            leaving[n] = leaving[n] * jnp.exp2(rates_s[n] * sum_cols[...])


class AdjointRows:
    def first(self, step_p, grad_p, rates, seg_cols, entering, read_p, rates_s, before_rows,
              before_cols, sum_cols, core, below, start_cols, seg, keep, give,
              scaled, leaving):
        leaving[...] = jnp.zeros_like(leaving)
        for n in range(scaled.shape[0]):
            scaled[n] = entering[n] * jnp.exp2(rates_s[n] * sum_cols[...])

    def main(self, b, step_p, grad_p, rates, seg_cols, entering, read_p, rates_s, before_rows,
             before_cols, sum_cols, core, below, start_cols, seg, keep, give,
             scaled, leaving):
        states = seg.shape[0]
        take(b, seg_cols, scaled, start_cols, False)

        def group(ns, d):
            r = [rates[n, d] for n in ns]
            passed_v = [[None] * BJ for _ in ns]
            for i in reversed(range(BI)):
                after = before_cols[i, d]
                for j in range(BJ):
                    after = after + step_p[i * BJ + j, d]
                passed = []
                for k, n in enumerate(ns):
                    passed.append(start_cols[n, i, d] * jnp.exp2(-r[k] * after))
                    start_cols[n, i, d] = passed[k]
                for j in reversed(range(BJ)):
                    p = i * BJ + j
                    c, g = step_p[p, d], grad_p[p, d]
                    for k, n in enumerate(ns):
                        decay = jnp.exp2(c * r[k])
                        adjoint = g * row_of(read_p, p, n) + passed[k]
                        passed[k] = decay * adjoint
                        if i == BI - 1:
                            passed_v[k][j] = passed[k]
                        else:
                            passed_v[k][j] = decay * (adjoint + passed_v[k][j])
            for j in range(BJ):
                before = before_rows[j, d]
                for k, n in enumerate(ns):
                    seg[n, j, d] = passed_v[k][j] * jnp.exp2(r[k] * before)

        each_group(b, states, 8, group)
        send(b, seg, below, leaving, True)

    def last(self, step_p, grad_p, rates, seg_cols, entering, read_p, rates_s, before_rows,
             before_cols, sum_cols, core, below, start_cols, seg, keep, give,
             scaled, leaving):
        part_by_core(core, leaving, keep, give)


class Final:
    def first(self, step_p, source_p, grad_p, rates, start_rows, start_cols, seg_s, seg_v,
              enter_s, keep, got, write_p, read_p, rates_v, before_rows, before_cols, sum_rows,
              core, features_p, steps_p, sum_w, sum_r, grad_decay,
              entering, decay_term):
        join_by_core(core, keep, got, entering)
        for n in range(entering.shape[0]):
            entering[n] = entering[n] * jnp.exp2(rates_v[n] * sum_rows[...])
        sum_w[...] = jnp.zeros_like(sum_w)
        sum_r[...] = jnp.zeros_like(sum_r)

    def main(self, b, step_p, source_p, grad_p, rates, start_rows, start_cols, seg_s, seg_v,
             enter_s, keep, got, write_p, read_p, rates_v, before_rows, before_cols, sum_rows,
             core, features_p, steps_p, sum_w, sum_r, grad_decay,
             entering, decay_term):
        states = rates.shape[0]
        take(b, seg_s, enter_s, seg_s, False)
        take(b, seg_v, entering, seg_v, True)
        at = block_of(b)
        features_p[:, at] = jnp.zeros((POS, BLOCK, LANES), F32)
        steps_p[:, at] = jnp.zeros((POS, BLOCK, LANES), F32)

        def group(ns, d):
            r = [rates[n, d] for n in ns]
            vert = [[start_rows[n, j, d] for j in range(BJ)] for n in ns]
            from_v, from_s = [{} for _ in ns], [{} for _ in ns]
            for i in range(BI):
                before = before_cols[i, d]
                state = [seg_s[n, i, d] * jnp.exp2(r[k] * before) for k, n in enumerate(ns)]
                for j in range(BJ):
                    p = i * BJ + j
                    c, s, g = step_p[p, d], source_p[p, d], grad_p[p, d]
                    for k, n in enumerate(ns):
                        decay = jnp.exp2(c * r[k])
                        dv = decay * vert[k][j]
                        vert[k][j] = dv + s * row_of(write_p, p, n)
                        ds = decay * state[k]
                        state[k] = ds + vert[k][j]
                        sum_r[p, pl.ds(n * 8, 8)] += state[k] * g
                        from_v[k][p] = dv
                        from_s[k][p] = ds
            passed_v = [[None] * BJ for _ in ns]
            for j in range(BJ):
                after = before_rows[j, d]
                for i in range(BI):
                    after = after + step_p[i * BJ + j, d]
                for k, n in enumerate(ns):
                    passed_v[k][j] = seg_v[n, j, d] * jnp.exp2(-r[k] * after)
            total = [None for _ in ns]
            for i in reversed(range(BI)):
                passed = [start_cols[n, i, d] for n in ns]
                for j in reversed(range(BJ)):
                    p = i * BJ + j
                    c, s, g = step_p[p, d], source_p[p, d], grad_p[p, d]
                    sum_q, sum_t = None, None
                    for k, n in enumerate(ns):
                        adjoint = g * row_of(read_p, p, n) + passed[k]
                        m = c * r[k]
                        decay = jnp.exp2(m)
                        passed[k] = decay * adjoint
                        adjoint_v = adjoint + passed_v[k][j]
                        passed_v[k][j] = decay * adjoint_v
                        q = (adjoint * from_s[k][p] + adjoint_v * from_v[k][p]) * m
                        total[k] = q if total[k] is None else total[k] + q
                        t = adjoint_v * row_of(write_p, p, n)
                        sum_q = q if sum_q is None else sum_q + q
                        sum_t = t if sum_t is None else sum_t + t
                        sum_w[p, pl.ds(n * 8, 8)] += adjoint_v * s
                    steps_p[p, d] += sum_q
                    features_p[p, d] += sum_t
            for k, n in enumerate(ns):
                decay_term[n, d] = total[k]

        each_group(b, states, 8, group)
        for p in range(POS):
            t, s = features_p[p, at], step_p[p, at]
            features_p[p, at] = s * t
            steps_p[p, at] = (source_p[p, at] * t + steps_p[p, at] * LN2) / s

    def last(self, step_p, source_p, grad_p, rates, start_rows, start_cols, seg_s, seg_v,
             enter_s, keep, got, write_p, read_p, rates_v, before_rows, before_cols, sum_rows,
             core, features_p, steps_p, sum_w, sum_r, grad_decay,
             entering, decay_term):
        for n in range(rates.shape[0]):
            out = lax.dot_general(
                jnp.ones((8, 2 * LANES), BF16), jnp.concatenate(halves(decay_term[n]), 1),
                (((1,), (1,)), ((), ())), preferred_element_type=F32,
            )
            grad_decay[pl.ds(n, 1)] = out[0:1] * LN2


class Unpack:
    def lead(self, i, features_p, steps_p, sum_w, sum_r, features, steps, writes, reads, turned):
        for j in range(BJ):
            for values, out in ((features_p, features), (steps_p, steps)):
                back = values[i * BJ + j].T
                for hs in range(HS):
                    out[hs, i, pl.ds(j, WS, stride=BJ), :] = back[hs * WS : hs * WS + WS]
        states = writes.shape[2]
        for values, out in ((sum_w, writes), (sum_r, reads)):
            for j in range(BJ):
                back = sum(values[i * BJ + j, pl.ds(k, states, stride=8), :] for k in range(8)).T
                for hs in range(HS):
                    turned[hs, pl.ds(j, WS, stride=BJ), :] = back[hs * WS : hs * WS + WS]
            for hs in range(HS):
                out[hs, i] = turned[hs].T


def prefix_kernel(held, sums, rates, out, *, reverse):
    size, share = out.shape[:2]
    at = sums.shape[1] - 1
    order = list(reversed(range(size))) if reverse else list(range(size))
    for n in range(share):
        before = jnp.zeros(out.shape[2:], F32)
        for k in order:
            out[k, n] = before
            before = jnp.exp2(rates[n] * sums[k, at]) * before + held[k, n]


def cut(ref, kind, k):
    if kind == "channels":
        index = (slice(None),) * (len(ref.shape) - 2) + (block_of(k),)
        return ref.at[index]
    if kind == "second":
        return ref.at[:, k]
    size = ref.shape[0] // BI
    return ref.at[pl.ds(k * size, size)]


def run(stage, ins, outs, scratch=(), micros=5):
    in_kinds, out_kinds = [k for _, k in ins], [k for _, k in outs]
    shapes = [a.shape for a, _ in ins] + [s for s, _ in outs]
    kinds = in_kinds + out_kinds
    streamed = [at for at, k in enumerate(kinds) if k not in ("whole", "scalar")]
    count = len(ins)

    def kernel(*refs):
        given = list(refs[: len(kinds)])
        rest = refs[len(kinds) :]
        buffers, sems = rest[: len(streamed)], rest[len(streamed)]
        extra = rest[len(streamed) + 1 :]
        views = list(given)
        copies = {}
        for slot, at in enumerate(streamed):
            views[at] = buffers[slot]

            def copy(k, slot=slot, at=at):
                far, near = cut(given[at], kinds[at], k), cut(buffers[slot], kinds[at], k)
                pair = (far, near) if at < count else (near, far)
                return pltpu.make_async_copy(*pair, sems.at[slot, k])

            copies[at] = copy

        def chosen(inputs, channels):
            return [
                copies[at] for at in streamed
                if (at < count) == inputs and (kinds[at] == "channels") == channels
            ]

        for channels in (False, True):
            for k in range(STEPS):
                for copy in chosen(True, channels):
                    copy(k).start()
        if hasattr(stage, "first"):
            stage.first(*views, *extra)
        for channels, part in ((False, "lead"), (True, "main")):
            def one(k, carry):
                for copy in chosen(True, channels):
                    copy(k).wait()
                if hasattr(stage, part):
                    getattr(stage, part)(k, *views, *extra)
                for copy in chosen(False, channels):
                    copy(k).start()
                return carry

            if hasattr(stage, part) or chosen(True, channels):
                lax.fori_loop(0, STEPS, one, 0)
        if hasattr(stage, "last"):
            stage.last(*views, *extra)
        for channels in (False, True):
            for k in range(STEPS):
                for copy in chosen(False, channels):
                    copy(k).wait()

    def spec(kind):
        if kind == "whole":
            return pl.BlockSpec(memory_space=pltpu.VMEM)
        if kind == "scalar":
            return pl.BlockSpec(memory_space=pltpu.SMEM)
        return pl.BlockSpec(memory_space=pl.ANY)

    return pl.pallas_call(
        kernel,
        out_shape=[jax.ShapeDtypeStruct(s, F32) for s, _ in outs],
        in_specs=[spec(k) for k in in_kinds],
        out_specs=[spec(k) for k in out_kinds],
        scratch_shapes=[pltpu.VMEM(shapes[at], F32) for at in streamed]
        + [pltpu.SemaphoreType.DMA((len(streamed), STEPS))]
        + [pltpu.VMEM(s, F32) for s in scratch],
        compiler_params=pltpu.CompilerParams(vmem_limit_bytes=60 << 20),
        cost_estimate=pl.CostEstimate(
            flops=0, bytes_accessed=int(micros * 3.3e6), transcendentals=0
        ),
    )(*[a for a, _ in ins])


def swap_cores(x, size):
    return lax.ppermute(x, "row", [(k, k ^ 1) for k in range(size)])


def tied(*arrays):
    return lax.optimization_barrier(arrays)


def row_total(keep, give, sums, other_sums, rates, size, reverse):
    count = keep.shape[0]
    core = lax.axis_index("row") % 2
    theirs = swap_cores(give, size)
    rate = lax.dynamic_slice_in_dim(rates, core * count, count, 0)
    first = core == (1 if reverse else 0)
    near = jnp.where(first, keep, theirs)
    far = jnp.where(first, theirs, keep)
    near_sum = jnp.where(first, sums, other_sums)
    far_sum = jnp.where(first, other_sums, sums)
    total = far + jnp.exp2(rate * far_sum) * near
    return total, near, near_sum, far_sum, rate


def row_carry(total, near, near_sum, far_sum, rate, beside, size, reverse):
    core = lax.axis_index("row") % 2
    first = core == (1 if reverse else 0)
    sign = -2 if reverse else 2

    def shift(x, by):
        return lax.ppermute(
            x, "row", [(k, k + by) for k in range(size) if 0 <= k + by < size]
        )

    entering = shift(total, sign)
    if size > 4:
        span = shift(near_sum + far_sum, sign)
        by = sign
        while abs(by) < size - 2:
            entering = entering + jnp.exp2(rate * span) * shift(entering, by)
            span = span + shift(span, by)
            by *= 2
    entering, _ = tied(entering, beside)
    to_far = near + jnp.exp2(rate * near_sum) * entering
    keep = jnp.where(first, entering, to_far)
    give = jnp.where(first, to_far, entering)
    return keep, swap_cores(give, size)


def col_gather(sent):
    return lax.all_to_all(sent, "col", 0, 0)


def col_carry(held, sums, rates, reverse):
    size, share = held.shape[0], rates.shape[0]
    vmem = pl.BlockSpec(memory_space=pltpu.VMEM)
    return pl.pallas_call(
        functools.partial(prefix_kernel, reverse=reverse),
        out_shape=jax.ShapeDtypeStruct((size, share) + held.shape[2:], F32),
        in_specs=[vmem] * 3,
        out_specs=vmem,
        compiler_params=pltpu.CompilerParams(vmem_limit_bytes=4 << 20),
    )(held, sums, rates)


def col_return(carries):
    back = lax.all_to_all(carries, "col", 0, 0)
    return back.reshape((-1,) + carries.shape[2:])


def total_of(x, rows, cols):
    by = 1
    while by < rows:
        x = x + lax.ppermute(x, "row", [(k, k ^ by) for k in range(rows)])
        by *= 2
    parts = lax.all_to_all(jnp.broadcast_to(x[None], (cols,) + x.shape), "col", 0, 0)
    return jnp.sum(parts, 0)


def shards(features, step_size, write_weights, read_weights, decay_log, out_grad, sizes):
    rows, cols = sizes
    states = decay_log.shape[0]
    share = states // cols
    tile_h, tile_w = features.shape[:2]
    orders = {k: jnp.asarray(v, BF16) for k, v in lane_orders().items()}
    plane, quad = (POS, D, LANES), (4, D, LANES)
    seg = (states, 4, D, LANES)
    all_rates = (states, D, LANES)
    small = (POS, states, LANES)
    packed = (HS, BI, tile_w, D)
    weights = (HS, BI, states, tile_w)
    turned = (HS, tile_w, states)
    size_v, size_s = (states, D // 2, LANES), (states, D // 4, LANES)
    half_v = (states // 2,) + size_v[1:]
    core = (lax.axis_index("row") % 2).astype(jnp.int32).reshape(1)
    place = lax.axis_index("col").astype(jnp.int32).reshape(1)

    (step_p, grad_p, rates, seg_cols, read_p, rates_v, rates_s, own_rates, before_cols, sum_cols,
     sum_rows, sent) = run(
        AdjointCols(),
        [(step_size.reshape(packed), "second"), (out_grad.reshape(packed), "second"),
         (read_weights.swapaxes(1, 2).reshape(weights), "second"),
         (decay_log.reshape(BI, states // BI, D), "whole"), (place, "scalar"),
         (orders["left"], "whole"), (orders["right"], "whole")],
        [(plane, "first"), (plane, "first"), (all_rates, "first"), (seg, "channels"),
         (small, "whole"), (size_v, "whole"), (size_s, "whole"), ((share,) + size_s[1:], "whole"),
         (quad, "whole"), (size_s[1:], "whole"), (size_v[1:], "whole"),
         ((cols, share + 1) + size_s[1:], "whole")],
        [turned, size_s],
    )
    held = col_gather(sent)
    other_rows = swap_cores(sum_rows, rows)
    step_p, _ = tied(step_p, sent)
    source_p, seg_rows, write_p, before_rows, keep, give = run(
        ForwardRows(),
        [(features.reshape(packed), "second"), (step_p, "first"), (rates, "channels"),
         (write_weights.swapaxes(1, 2).reshape(weights), "second"), (rates_v, "whole"),
         (sum_rows, "whole"), (core, "scalar"), (orders["above"], "whole")],
        [(plane, "first"), (seg, "channels"), (small, "whole"), (quad, "whole"),
         (half_v, "whole"), (half_v, "whole")],
        [turned, size_v],
    )
    total = row_total(keep, give, sum_rows, other_rows, rates_v, rows, False)
    held, first = tied(held, total[0])
    col_sums = held
    carries = col_carry(held, held, own_rates, True)
    enter_cols = col_return(carries)
    keep, got = row_carry(first, *total[1:], carries, rows, False)
    start_rows, seg_s, leave_s = run(
        ForwardCols(),
        [(step_p, "channels"), (source_p, "channels"), (rates, "channels"),
         (seg_rows, "channels"), (keep, "whole"), (got, "whole"), (write_p, "whole"),
         (rates_s, "whole"), (before_rows, "whole"), (before_cols, "whole"),
         (sum_cols, "whole"), (core, "scalar"), (orders["left"], "whole")],
        [(seg, "channels"), (seg, "channels"), (size_s, "whole")], [size_v], 10,
    )
    held = col_gather(leave_s.reshape((cols, share) + size_s[1:]))
    enter_cols, _ = tied(enter_cols, leave_s)
    start_cols, seg_v, keep, give = run(
        AdjointRows(),
        [(step_p, "channels"), (grad_p, "channels"), (rates, "channels"),
         (seg_cols, "channels"), (enter_cols, "whole"), (read_p, "whole"), (rates_s, "whole"),
         (before_rows, "whole"), (before_cols, "whole"), (sum_cols, "whole"), (core, "scalar"),
         (orders["below"], "whole")],
        [(seg, "channels"), (seg, "channels"), (half_v, "whole"), (half_v, "whole")],
        [size_s, size_v], 10,
    )
    held, give = tied(held, give)
    carries = col_carry(held, col_sums, own_rates, False)
    enter_s = col_return(carries)
    total = row_total(keep, give, sum_rows, other_rows, rates_v, rows, True)
    keep, got = row_carry(*total, enter_s, rows, True)
    features_p, steps_p, sum_w, sum_r, grad_decay = run(
        Final(),
        [(step_p, "channels"), (source_p, "channels"), (grad_p, "channels"),
         (rates, "channels"), (start_rows, "channels"), (start_cols, "channels"),
         (seg_s, "channels"), (seg_v, "channels"), (enter_s, "whole"), (keep, "whole"),
         (got, "whole"), (write_p, "whole"), (read_p, "whole"), (rates_v, "whole"),
         (before_rows, "whole"), (before_cols, "whole"), (sum_rows, "whole"), (core, "scalar")],
        [(plane, "channels"), (plane, "channels"), ((POS, states * 8, LANES), "whole"),
         ((POS, states * 8, LANES), "whole"), ((states, D), "whole")],
        [size_v, all_rates], 25,
    )
    grad_decay = total_of(grad_decay, rows, cols)
    grad_features, grad_step, grad_write, grad_read = run(
        Unpack(),
        [(features_p, "first"), (steps_p, "first"), (sum_w, "first"), (sum_r, "first")],
        [(packed, "second"), (packed, "second"), (weights, "second"), (weights, "second")],
        [turned],
    )
    weights = (tile_h, states, tile_w)
    return (
        grad_features.reshape(features.shape),
        grad_step.reshape(features.shape),
        grad_write.reshape(weights).swapaxes(1, 2),
        grad_read.reshape(weights).swapaxes(1, 2),
        grad_decay,
    )


def solution(mesh):
    spec = P("row", "col", None)
    sizes = (mesh.shape["row"], mesh.shape["col"])
    return jax.shard_map(
        functools.partial(shards, sizes=sizes),
        mesh=mesh,
        in_specs=(spec, spec, spec, spec, P(), spec),
        out_specs=(spec, spec, spec, spec, P()),
        check_vma=False,
    )
```

```python
import functools

import jax
import jax.numpy as jnp
import numpy as np
from jax import lax
from jax.experimental import pallas as pl
from jax.experimental.pallas import tpu as pltpu
from jax.sharding import PartitionSpec as P

HS, WS, BI, BJ = 8, 16, 4, 4
POS = BI * BJ
LANES = 128
D = 128
STEPS = 4
BLOCK = D // STEPS
F32 = jnp.float32
BF16 = jnp.bfloat16
LOG2E = 1.4426950408889634
LN2 = 0.6931471805599453


@functools.cache
def lane_orders():
    lane = np.arange(LANES)
    hs, ws = lane // WS, lane % WS
    same_w = ws[:, None] == ws[None]
    same_h = hs[:, None] == hs[None]
    out = {
        "above": same_w & (hs[:, None] < hs[None]), "below": same_w & (hs[:, None] > hs[None]),
        "left": same_h & (ws[:, None] < ws[None]), "right": same_h & (ws[:, None] > ws[None]),
    }
    return {k: np.concatenate([v, v], 0).astype(np.float32) for k, v in out.items()}


def lane_places(rows, out):
    at = lax.broadcasted_iota(jnp.int32, (2 * LANES, LANES), 0) % LANES
    lane = lax.broadcasted_iota(jnp.int32, (2 * LANES, LANES), 1)
    segment, edge = (at, lane) if out else (lane, at)
    return edge - (segment % WS if rows else segment // WS)


def edge_start(b, k, rows):
    return (b // 2) * 64 + k * WS if rows else b * 32 + k * HS


def placed(places, start):
    return jnp.where(places == start, 1.0, 0.0).astype(BF16)


def halves(x):
    high = x.astype(BF16)
    low = (x - high.astype(F32)).astype(BF16)
    return high, low


def lane_dot(matrix, *parts):
    parts = [h for x in parts for h in halves(x)]
    return jnp.dot(jnp.concatenate(parts, 1), matrix, preferred_element_type=F32)


def lane_dot_exact(x, matrix):
    high, low = halves(x)
    rest = (x - high.astype(F32) - low.astype(F32)).astype(BF16)
    return jnp.dot(
        jnp.concatenate([high, low], 1), matrix, preferred_element_type=F32
    ) + jnp.dot(rest, matrix[:LANES], preferred_element_type=F32)


def row_of(ref, p, n):
    return jnp.broadcast_to(ref[p, pl.ds(n, 1), :], (8, LANES))


def block_of(b):
    return pl.ds(pl.multiple_of(b * BLOCK, BLOCK), BLOCK)


def half_of(b):
    return pl.ds(pl.multiple_of((b % 2) * BLOCK, BLOCK), BLOCK)


def each_group(b, states, size, body):
    groups = states // size

    def one(at, carry):
        d = pl.ds(pl.multiple_of(b * BLOCK + (at // groups) * 8, 8), 8)
        body([(at % groups) * size + k for k in range(size)], d)
        return carry

    lax.fori_loop(0, (BLOCK // 8) * groups, one, 0)


def send(b, seg, order, leaving, rows):
    states = seg.shape[0]
    at = block_of(b)
    total = None
    places = lane_places(rows, True)
    for k in range(4):
        matrix = jnp.concatenate([placed(places, edge_start(b, k, rows)), order[...]], 1)
        both = lane_dot(matrix, seg[:, k, at].reshape(states * BLOCK, LANES))
        seg[:, k, at] = both[:, LANES:].reshape(states, BLOCK, LANES)
        total = both[:, :LANES] if total is None else total + both[:, :LANES]
    total = total.reshape(states, BLOCK, LANES)
    if rows:
        leaving[:, half_of(b)] += total
    else:
        leaving[...] += total


def take(b, seg, entering, out, rows):
    states = seg.shape[0]
    entering = entering[:, half_of(b)] if rows else entering[...]
    places = lane_places(rows, False)
    matrix = jnp.concatenate([placed(places, edge_start(b, k, rows)) for k in range(4)], 1)
    first = lane_dot(matrix, entering.reshape(states * BLOCK, LANES))
    at = block_of(b)
    for k in range(4):
        out[:, k, at] = seg[:, k, at] + first[:, k * LANES : (k + 1) * LANES].reshape(
            states, BLOCK, LANES
        )


def part_by_core(core, whole, keep, give):
    count = whole.shape[0] // 2
    for n in range(count):
        low, high = whole[n], whole[count + n]
        keep[n] = jnp.where(core[0] == 0, low, high)
        give[n] = jnp.where(core[0] == 0, high, low)


def join_by_core(core, keep, got, whole):
    count = whole.shape[0] // 2
    for n in range(count):
        whole[n] = jnp.where(core[0] == 0, keep[n], got[n])
        whole[count + n] = jnp.where(core[0] == 0, got[n], keep[n])


def gather_plane(ref, i, j):
    return jnp.concatenate([ref[hs, i, pl.ds(j, WS, stride=BJ), :] for hs in range(HS)], 0).T


def gather_states(ref, i, turned, out):
    for hs in range(HS):
        turned[hs] = ref[hs, i].T
    for j in range(BJ):
        out[i * BJ + j] = jnp.concatenate(
            [turned[hs, pl.ds(j, WS, stride=BJ), :] for hs in range(HS)], 0
        ).T


def pack_rates(i, decay_log, rates, rates_v, rates_s):
    lane = lax.broadcasted_iota(jnp.int32, (BLOCK, LANES), 1)
    lane_v = lax.broadcasted_iota(jnp.int32, (2 * BLOCK, LANES), 1)
    rate = (-LOG2E * jnp.exp(decay_log[i])).T
    count = rates.shape[0] // BI
    for k in range(count):
        n = i * count + k
        r = jnp.broadcast_to(rate[:, k : k + 1], (D, LANES))
        rates[n] = r
        part = [r[q * BLOCK : (q + 1) * BLOCK] for q in range(4)]
        rates_v[n] = jnp.where(lane_v < 64, r[: 2 * BLOCK], r[2 * BLOCK :])
        rates_s[n] = jnp.where(
            lane < 64, jnp.where(lane < 32, part[0], part[1]),
            jnp.where(lane < 96, part[2], part[3]),
        )


class AdjointCols:
    def first(self, step, grad, read, decay_log, place, left, right,
              step_p, grad_p, rates, seg, read_p, rates_v, rates_s, own_rates, before_cols,
              sum_cols, sum_rows, sent, turned, leaving):
        sum_cols[...] = jnp.zeros_like(sum_cols)
        leaving[...] = jnp.zeros_like(leaving)

    def lead(self, i, step, grad, read, decay_log, place, left, right,
             step_p, grad_p, rates, seg, read_p, rates_v, rates_s, own_rates, before_cols,
             sum_cols, sum_rows, sent, turned, leaving):
        row_total = None
        for j in range(BJ):
            s = gather_plane(step, i, j)
            step_p[i * BJ + j] = s
            grad_p[i * BJ + j] = gather_plane(grad, i, j)
            row_total = s if row_total is None else row_total + s
        gather_states(read, i, turned, read_p)
        pack_rates(i, decay_log, rates, rates_v, rates_s)
        before_cols[i] = lane_dot_exact(row_total, left[...])
        places = lane_places(False, True)
        for q in range(STEPS):
            sum_cols[...] += lane_dot_exact(
                row_total[q * BLOCK : (q + 1) * BLOCK], placed(places, edge_start(q, i, False))
            )

    def main(self, b, step, grad, read, decay_log, place, left, right,
             step_p, grad_p, rates, seg, read_p, rates_v, rates_s, own_rates, before_cols,
             sum_cols, sum_rows, sent, turned, leaving):
        states = seg.shape[0]

        def group(ns, d):
            r = [rates[n, d] for n in ns]
            for i in range(BI):
                acc = [None] * len(ns)
                c = before_cols[i, d]
                for j in range(BJ):
                    p = i * BJ + j
                    c = c + step_p[p, d]
                    g = grad_p[p, d]
                    for k, n in enumerate(ns):
                        term = jnp.exp2(c * r[k]) * g * row_of(read_p, p, n)
                        acc[k] = term if acc[k] is None else acc[k] + term
                for k, n in enumerate(ns):
                    seg[n, i, d] = acc[k]

        each_group(b, states, 16, group)
        send(b, seg, right, leaving, False)

    def last(self, step, grad, read, decay_log, place, left, right,
             step_p, grad_p, rates, seg, read_p, rates_v, rates_s, own_rates, before_cols,
             sum_cols, sum_rows, sent, turned, leaving):
        share = own_rates.shape[0]
        for k in range(sent.shape[0]):
            sent[k, 0:share] = leaving[k * share : (k + 1) * share]
            sent[k, share] = sum_cols[...]
        for k in range(share):
            own_rates[k] = rates_s[place[0] * share + k]
        places = lane_places(True, True)
        for r in range(2):
            total = None
            for q in (r, r + 2):
                for j in range(BJ):
                    run = None
                    for i in range(BI):
                        s = step_p[i * BJ + j, q * BLOCK : (q + 1) * BLOCK]
                        run = s if run is None else run + s
                    one = lane_dot_exact(run, placed(places, edge_start(q, j, True)))
                    total = one if total is None else total + one
            sum_rows[r * BLOCK : (r + 1) * BLOCK] = total


class ForwardRows:
    def first(self, feat, step_p, rates, write, rates_v, sum_rows, core, above,
              source_p, seg, write_p, before_rows, keep, give, turned, leaving):
        leaving[...] = jnp.zeros_like(leaving)

    def lead(self, i, feat, step_p, rates, write, rates_v, sum_rows, core, above,
             source_p, seg, write_p, before_rows, keep, give, turned, leaving):
        for j in range(BJ):
            source_p[i * BJ + j] = step_p[i * BJ + j] * gather_plane(feat, i, j)
        gather_states(write, i, turned, write_p)

        @pl.when(i == BI - 1)
        def _():
            for j in range(BJ):
                run = step_p[j]
                for k in range(1, BI):
                    run = run + step_p[k * BJ + j]
                before_rows[j] = lane_dot_exact(run, above[...])

    def main(self, b, feat, step_p, rates, write, rates_v, sum_rows, core, above,
             source_p, seg, write_p, before_rows, keep, give, turned, leaving):
        states = seg.shape[0]

        def group(ns, d):
            r = [-rates[n, d] for n in ns]
            for j in range(BJ):
                acc = [None] * len(ns)
                c = before_rows[j, d]
                for i in range(BI):
                    p = i * BJ + j
                    c = c + step_p[p, d]
                    s = source_p[p, d]
                    for k, n in enumerate(ns):
                        term = jnp.exp2(c * r[k]) * s * row_of(write_p, p, n)
                        acc[k] = term if acc[k] is None else acc[k] + term
                for k, n in enumerate(ns):
                    seg[n, j, d] = acc[k]

        each_group(b, states, 16, group)
        send(b, seg, above, leaving, True)

    def last(self, feat, step_p, rates, write, rates_v, sum_rows, core, above,
             source_p, seg, write_p, before_rows, keep, give, turned, leaving):
        for n in range(leaving.shape[0]):
            leaving[n] = leaving[n] * jnp.exp2(rates_v[n] * sum_rows[...])
        part_by_core(core, leaving, keep, give)


class ForwardCols:
    def first(self, step_p, source_p, rates, seg_rows, keep, got, write_p, rates_s, before_rows,
              before_cols, sum_cols, core, left, start_rows, seg, leaving, entering):
        leaving[...] = jnp.zeros_like(leaving)
        join_by_core(core, keep, got, entering)

    def main(self, b, step_p, source_p, rates, seg_rows, keep, got, write_p, rates_s, before_rows,
             before_cols, sum_cols, core, left, start_rows, seg, leaving, entering):
        states = seg.shape[0]
        take(b, seg_rows, entering, start_rows, True)

        def group(ns, d):
            r = [rates[n, d] for n in ns]
            vert = [[None] * BJ for _ in ns]
            for j in range(BJ):
                before = before_rows[j, d]
                for k, n in enumerate(ns):
                    vert[k][j] = start_rows[n, j, d] * jnp.exp2(r[k] * before)
                    start_rows[n, j, d] = vert[k][j]
            for i in range(BI):
                state = [None] * len(ns)
                after = before_cols[i, d]
                for j in range(BJ):
                    p = i * BJ + j
                    c, s = step_p[p, d], source_p[p, d]
                    after = after + c
                    for k, n in enumerate(ns):
                        decay = jnp.exp2(c * r[k])
                        vert[k][j] = decay * vert[k][j] + s * row_of(write_p, p, n)
                        state[k] = vert[k][j] if j == 0 else decay * state[k] + vert[k][j]
                for k, n in enumerate(ns):
                    seg[n, i, d] = state[k] * jnp.exp2(-r[k] * after)

        each_group(b, states, 8, group)
        send(b, seg, left, leaving, False)

    def last(self, step_p, source_p, rates, seg_rows, keep, got, write_p, rates_s, before_rows,
             before_cols, sum_cols, core, left, start_rows, seg, leaving, entering):
        for n in range(leaving.shape[0]):
            leaving[n] = leaving[n] * jnp.exp2(rates_s[n] * sum_cols[...])


class AdjointRows:
    def first(self, step_p, grad_p, rates, seg_cols, entering, read_p, rates_s, before_rows,
              before_cols, sum_cols, core, below, start_cols, seg, keep, give,
              scaled, leaving):
        leaving[...] = jnp.zeros_like(leaving)
        for n in range(scaled.shape[0]):
            scaled[n] = entering[n] * jnp.exp2(rates_s[n] * sum_cols[...])

    def main(self, b, step_p, grad_p, rates, seg_cols, entering, read_p, rates_s, before_rows,
             before_cols, sum_cols, core, below, start_cols, seg, keep, give,
             scaled, leaving):
        states = seg.shape[0]
        take(b, seg_cols, scaled, start_cols, False)

        def group(ns, d):
            r = [rates[n, d] for n in ns]
            passed_v = [[None] * BJ for _ in ns]
            for i in reversed(range(BI)):
                after = before_cols[i, d]
                for j in range(BJ):
                    after = after + step_p[i * BJ + j, d]
                passed = []
                for k, n in enumerate(ns):
                    passed.append(start_cols[n, i, d] * jnp.exp2(-r[k] * after))
                    start_cols[n, i, d] = passed[k]
                for j in reversed(range(BJ)):
                    p = i * BJ + j
                    c, g = step_p[p, d], grad_p[p, d]
                    for k, n in enumerate(ns):
                        decay = jnp.exp2(c * r[k])
                        adjoint = g * row_of(read_p, p, n) + passed[k]
                        passed[k] = decay * adjoint
                        if i == BI - 1:
                            passed_v[k][j] = passed[k]
                        else:
                            passed_v[k][j] = decay * (adjoint + passed_v[k][j])
            for j in range(BJ):
                before = before_rows[j, d]
                for k, n in enumerate(ns):
                    seg[n, j, d] = passed_v[k][j] * jnp.exp2(r[k] * before)

        each_group(b, states, 8, group)
        send(b, seg, below, leaving, True)

    def last(self, step_p, grad_p, rates, seg_cols, entering, read_p, rates_s, before_rows,
             before_cols, sum_cols, core, below, start_cols, seg, keep, give,
             scaled, leaving):
        part_by_core(core, leaving, keep, give)


class Final:
    def first(self, step_p, source_p, grad_p, rates, start_rows, start_cols, seg_s, seg_v,
              enter_s, keep, got, write_p, read_p, rates_v, before_rows, before_cols, sum_rows,
              core, features_p, steps_p, sum_w, sum_r, grad_decay,
              entering, decay_term):
        join_by_core(core, keep, got, entering)
        for n in range(entering.shape[0]):
            entering[n] = entering[n] * jnp.exp2(rates_v[n] * sum_rows[...])
        sum_w[...] = jnp.zeros_like(sum_w)
        sum_r[...] = jnp.zeros_like(sum_r)

    def main(self, b, step_p, source_p, grad_p, rates, start_rows, start_cols, seg_s, seg_v,
             enter_s, keep, got, write_p, read_p, rates_v, before_rows, before_cols, sum_rows,
             core, features_p, steps_p, sum_w, sum_r, grad_decay,
             entering, decay_term):
        states = rates.shape[0]
        take(b, seg_s, enter_s, seg_s, False)
        take(b, seg_v, entering, seg_v, True)
        at = block_of(b)
        features_p[:, at] = jnp.zeros((POS, BLOCK, LANES), F32)
        steps_p[:, at] = jnp.zeros((POS, BLOCK, LANES), F32)

        def group(ns, d):
            r = [rates[n, d] for n in ns]
            vert = [[start_rows[n, j, d] for j in range(BJ)] for n in ns]
            from_v, from_s = [{} for _ in ns], [{} for _ in ns]
            exps = [{} for _ in ns]
            for i in range(BI):
                before = before_cols[i, d]
                state = [seg_s[n, i, d] * jnp.exp2(r[k] * before) for k, n in enumerate(ns)]
                for j in range(BJ):
                    p = i * BJ + j
                    c, s, g = step_p[p, d], source_p[p, d], grad_p[p, d]
                    for k, n in enumerate(ns):
                        m = c * r[k]
                        decay = jnp.exp2(m)
                        dv = decay * vert[k][j]
                        vert[k][j] = dv + s * row_of(write_p, p, n)
                        ds = decay * state[k]
                        state[k] = ds + vert[k][j]
                        sum_r[p, pl.ds(n * 8, 8)] += state[k] * g
                        from_v[k][p] = dv
                        from_s[k][p] = ds
                        exps[k][p] = m
            passed_v = [[None] * BJ for _ in ns]
            for j in range(BJ):
                after = before_rows[j, d]
                for i in range(BI):
                    after = after + step_p[i * BJ + j, d]
                for k, n in enumerate(ns):
                    passed_v[k][j] = seg_v[n, j, d] * jnp.exp2(-r[k] * after)
            total = [None for _ in ns]
            for i in reversed(range(BI)):
                passed = [start_cols[n, i, d] for n in ns]
                for j in reversed(range(BJ)):
                    p = i * BJ + j
                    s, g = source_p[p, d], grad_p[p, d]
                    sum_q, sum_t = None, None
                    for k, n in enumerate(ns):
                        adjoint = g * row_of(read_p, p, n) + passed[k]
                        m = exps[k][p]
                        decay = jnp.exp2(m)
                        passed[k] = decay * adjoint
                        adjoint_v = adjoint + passed_v[k][j]
                        passed_v[k][j] = decay * adjoint_v
                        q = (adjoint * from_s[k][p] + adjoint_v * from_v[k][p]) * m
                        total[k] = q if total[k] is None else total[k] + q
                        t = adjoint_v * row_of(write_p, p, n)
                        sum_q = q if sum_q is None else sum_q + q
                        sum_t = t if sum_t is None else sum_t + t
                        sum_w[p, pl.ds(n * 8, 8)] += adjoint_v * s
                    steps_p[p, d] += sum_q
                    features_p[p, d] += sum_t
            for k, n in enumerate(ns):
                decay_term[n, d] = total[k]

        each_group(b, states, 8, group)
        for p in range(POS):
            t, s = features_p[p, at], step_p[p, at]
            features_p[p, at] = s * t
            steps_p[p, at] = (source_p[p, at] * t + steps_p[p, at] * LN2) / s

    def last(self, step_p, source_p, grad_p, rates, start_rows, start_cols, seg_s, seg_v,
             enter_s, keep, got, write_p, read_p, rates_v, before_rows, before_cols, sum_rows,
             core, features_p, steps_p, sum_w, sum_r, grad_decay,
             entering, decay_term):
        for n in range(rates.shape[0]):
            out = lax.dot_general(
                jnp.ones((8, 2 * LANES), BF16), jnp.concatenate(halves(decay_term[n]), 1),
                (((1,), (1,)), ((), ())), preferred_element_type=F32,
            )
            grad_decay[pl.ds(n, 1)] = out[0:1] * LN2


class Unpack:
    def lead(self, i, features_p, steps_p, sum_w, sum_r, features, steps, writes, reads, turned):
        for j in range(BJ):
            for values, out in ((features_p, features), (steps_p, steps)):
                back = values[i * BJ + j].T
                for hs in range(HS):
                    out[hs, i, pl.ds(j, WS, stride=BJ), :] = back[hs * WS : hs * WS + WS]
        states = writes.shape[2]
        for values, out in ((sum_w, writes), (sum_r, reads)):
            for j in range(BJ):
                back = sum(values[i * BJ + j, pl.ds(k, states, stride=8), :] for k in range(8)).T
                for hs in range(HS):
                    turned[hs, pl.ds(j, WS, stride=BJ), :] = back[hs * WS : hs * WS + WS]
            for hs in range(HS):
                out[hs, i] = turned[hs].T


def prefix_kernel(held, sums, rates, out, *, reverse):
    size, share = out.shape[:2]
    at = sums.shape[1] - 1
    order = list(reversed(range(size))) if reverse else list(range(size))
    for n in range(share):
        before = jnp.zeros(out.shape[2:], F32)
        for k in order:
            out[k, n] = before
            before = jnp.exp2(rates[n] * sums[k, at]) * before + held[k, n]


def cut(ref, kind, k):
    if kind == "channels":
        index = (slice(None),) * (len(ref.shape) - 2) + (block_of(k),)
        return ref.at[index]
    if kind == "second":
        return ref.at[:, k]
    size = ref.shape[0] // BI
    return ref.at[pl.ds(k * size, size)]


def run(stage, ins, outs, scratch=(), micros=5):
    in_kinds, out_kinds = [k for _, k in ins], [k for _, k in outs]
    shapes = [a.shape for a, _ in ins] + [s for s, _ in outs]
    types = [a.dtype for a, _ in ins] + [F32 for _ in outs]
    kinds = in_kinds + out_kinds
    phase = {"whole": 0, "second": 1, "first": 1, "channels": 2}
    copied = [at for at, k in enumerate(kinds) if k in phase]
    count = len(ins)

    def kernel(*refs):
        given = list(refs[: len(kinds)])
        rest = refs[len(kinds) :]
        buffers, sems = rest[: len(copied)], rest[len(copied)]
        extra = rest[len(copied) + 1 :]
        views = list(given)
        into, out_of = [[], [], []], [[], [], []]
        for slot, at in enumerate(copied):
            views[at] = buffers[slot]

            def copy(k, slot=slot, at=at):
                far, near = given[at], buffers[slot]
                if kinds[at] != "whole":
                    far, near = cut(far, kinds[at], k), cut(near, kinds[at], k)
                pair = (far, near) if at < count else (near, far)
                return pltpu.make_async_copy(*pair, sems.at[slot, k])

            (into if at < count else out_of)[phase[kinds[at]]].append(copy)

        def part(which, name):
            def one(k, carry):
                for copy in into[which]:
                    copy(k).wait()
                getattr(stage, name)(k, *views, *extra)
                for copy in out_of[which]:
                    copy(k).start()
                return carry

            lax.fori_loop(0, STEPS, one, 0)

        for which in range(3):
            for k in range(STEPS if which else 1):
                for copy in into[which]:
                    copy(k).start()
        for copy in into[0]:
            copy(0).wait()
        if hasattr(stage, "first"):
            stage.first(*views, *extra)
        if hasattr(stage, "lead"):
            part(1, "lead")
        if hasattr(stage, "main"):
            part(2, "main")
        if hasattr(stage, "last"):
            stage.last(*views, *extra)
        for copy in out_of[0]:
            copy(0).start()
        for which in range(3):
            for k in range(STEPS if which else 1):
                for copy in out_of[which]:
                    copy(k).wait()

    def spec(kind):
        if kind == "small":
            return pl.BlockSpec(memory_space=pltpu.VMEM)
        if kind == "scalar":
            return pl.BlockSpec(memory_space=pltpu.SMEM)
        return pl.BlockSpec(memory_space=pl.ANY)

    return pl.pallas_call(
        kernel,
        out_shape=[jax.ShapeDtypeStruct(s, F32) for s, _ in outs],
        in_specs=[spec(k) for k in in_kinds],
        out_specs=[spec(k) for k in out_kinds],
        scratch_shapes=[pltpu.VMEM(shapes[at], types[at]) for at in copied]
        + [pltpu.SemaphoreType.DMA((len(copied), STEPS))]
        + [pltpu.VMEM(s, F32) for s in scratch],
        compiler_params=pltpu.CompilerParams(vmem_limit_bytes=60 << 20),
        cost_estimate=pl.CostEstimate(
            flops=0, bytes_accessed=int(micros * 3.3e6), transcendentals=0
        ),
    )(*[a for a, _ in ins])


def swap_cores(x, size):
    return lax.ppermute(x, "row", [(k, k ^ 1) for k in range(size)])


def tied(*arrays):
    return lax.optimization_barrier(arrays)


def row_total(keep, give, sums, other_sums, rates, size, reverse):
    count = keep.shape[0]
    core = lax.axis_index("row") % 2
    theirs = swap_cores(give, size)
    rate = lax.dynamic_slice_in_dim(rates, core * count, count, 0)
    first = core == (1 if reverse else 0)
    near = jnp.where(first, keep, theirs)
    far = jnp.where(first, theirs, keep)
    near_sum = jnp.where(first, sums, other_sums)
    far_sum = jnp.where(first, other_sums, sums)
    total = far + jnp.exp2(rate * far_sum) * near
    return total, near, near_sum, far_sum, rate


def row_carry(total, near, near_sum, far_sum, rate, beside, size, reverse):
    core = lax.axis_index("row") % 2
    first = core == (1 if reverse else 0)
    sign = -2 if reverse else 2

    def shift(x, by):
        return lax.ppermute(
            x, "row", [(k, k + by) for k in range(size) if 0 <= k + by < size]
        )

    entering = shift(total, sign)
    if size > 4:
        span = shift(near_sum + far_sum, sign)
        by = sign
        while abs(by) < size - 2:
            entering = entering + jnp.exp2(rate * span) * shift(entering, by)
            span = span + shift(span, by)
            by *= 2
    entering, _ = tied(entering, beside)
    to_far = near + jnp.exp2(rate * near_sum) * entering
    keep = jnp.where(first, entering, to_far)
    give = jnp.where(first, to_far, entering)
    return keep, swap_cores(give, size)


def col_gather(sent):
    return lax.all_to_all(sent, "col", 0, 0)


def col_carry(held, sums, rates, reverse):
    size, share = held.shape[0], rates.shape[0]
    vmem = pl.BlockSpec(memory_space=pltpu.VMEM)
    return pl.pallas_call(
        functools.partial(prefix_kernel, reverse=reverse),
        out_shape=jax.ShapeDtypeStruct((size, share) + held.shape[2:], F32),
        in_specs=[vmem] * 3,
        out_specs=vmem,
        compiler_params=pltpu.CompilerParams(vmem_limit_bytes=4 << 20),
    )(held, sums, rates)


def col_return(carries):
    back = lax.all_to_all(carries, "col", 0, 0)
    return back.reshape((-1,) + carries.shape[2:])


def total_of(x, rows, cols):
    by = 1
    while by < rows:
        x = x + lax.ppermute(x, "row", [(k, k ^ by) for k in range(rows)])
        by *= 2
    parts = lax.all_to_all(jnp.broadcast_to(x[None], (cols,) + x.shape), "col", 0, 0)
    return jnp.sum(parts, 0)


def shards(features, step_size, write_weights, read_weights, decay_log, out_grad, sizes):
    rows, cols = sizes
    states = decay_log.shape[0]
    share = states // cols
    tile_h, tile_w = features.shape[:2]
    orders = {k: jnp.asarray(v, BF16) for k, v in lane_orders().items()}
    plane, quad = (POS, D, LANES), (4, D, LANES)
    seg = (states, 4, D, LANES)
    all_rates = (states, D, LANES)
    small = (POS, states, LANES)
    packed = (HS, BI, tile_w, D)
    weights = (HS, BI, states, tile_w)
    turned = (HS, tile_w, states)
    size_v, size_s = (states, D // 2, LANES), (states, D // 4, LANES)
    half_v = (states // 2,) + size_v[1:]
    core = (lax.axis_index("row") % 2).astype(jnp.int32).reshape(1)
    place = lax.axis_index("col").astype(jnp.int32).reshape(1)

    (step_p, grad_p, rates, seg_cols, read_p, rates_v, rates_s, own_rates, before_cols, sum_cols,
     sum_rows, sent) = run(
        AdjointCols(),
        [(step_size.reshape(packed), "second"), (out_grad.reshape(packed), "second"),
         (read_weights.swapaxes(1, 2).reshape(weights), "second"),
         (decay_log.reshape(BI, states // BI, D), "small"), (place, "scalar"),
         (orders["left"], "whole"), (orders["right"], "whole")],
        [(plane, "first"), (plane, "first"), (all_rates, "first"), (seg, "channels"),
         (small, "whole"), (size_v, "whole"), (size_s, "whole"), ((share,) + size_s[1:], "whole"),
         (quad, "whole"), (size_s[1:], "whole"), (size_v[1:], "whole"),
         ((cols, share + 1) + size_s[1:], "whole")],
        [turned, size_s],
    )
    held = col_gather(sent)
    other_rows = swap_cores(sum_rows, rows)
    step_p, _ = tied(step_p, sent)
    source_p, seg_rows, write_p, before_rows, keep, give = run(
        ForwardRows(),
        [(features.reshape(packed), "second"), (step_p, "first"), (rates, "channels"),
         (write_weights.swapaxes(1, 2).reshape(weights), "second"), (rates_v, "whole"),
         (sum_rows, "whole"), (core, "scalar"), (orders["above"], "whole")],
        [(plane, "first"), (seg, "channels"), (small, "whole"), (quad, "whole"),
         (half_v, "whole"), (half_v, "whole")],
        [turned, size_v],
    )
    total = row_total(keep, give, sum_rows, other_rows, rates_v, rows, False)
    held, first = tied(held, total[0])
    col_sums = held
    carries = col_carry(held, held, own_rates, True)
    enter_cols = col_return(carries)
    keep, got = row_carry(first, *total[1:], carries, rows, False)
    start_rows, seg_s, leave_s = run(
        ForwardCols(),
        [(step_p, "channels"), (source_p, "channels"), (rates, "channels"),
         (seg_rows, "channels"), (keep, "whole"), (got, "whole"), (write_p, "whole"),
         (rates_s, "whole"), (before_rows, "whole"), (before_cols, "whole"),
         (sum_cols, "whole"), (core, "scalar"), (orders["left"], "whole")],
        [(seg, "channels"), (seg, "channels"), (size_s, "whole")], [size_v], 10,
    )
    held = col_gather(leave_s.reshape((cols, share) + size_s[1:]))
    enter_cols, _ = tied(enter_cols, leave_s)
    start_cols, seg_v, keep, give = run(
        AdjointRows(),
        [(step_p, "channels"), (grad_p, "channels"), (rates, "channels"),
         (seg_cols, "channels"), (enter_cols, "whole"), (read_p, "whole"), (rates_s, "whole"),
         (before_rows, "whole"), (before_cols, "whole"), (sum_cols, "whole"), (core, "scalar"),
         (orders["below"], "whole")],
        [(seg, "channels"), (seg, "channels"), (half_v, "whole"), (half_v, "whole")],
        [size_s, size_v], 10,
    )
    held, give = tied(held, give)
    total = row_total(keep, give, sum_rows, other_rows, rates_v, rows, True)
    held, first = tied(held, total[0])
    carries = col_carry(held, col_sums, own_rates, False)
    enter_s = col_return(carries)
    keep, got = row_carry(first, *total[1:], carries, rows, True)
    features_p, steps_p, sum_w, sum_r, grad_decay = run(
        Final(),
        [(step_p, "channels"), (source_p, "channels"), (grad_p, "channels"),
         (rates, "channels"), (start_rows, "channels"), (start_cols, "channels"),
         (seg_s, "channels"), (seg_v, "channels"), (enter_s, "whole"), (keep, "whole"),
         (got, "whole"), (write_p, "whole"), (read_p, "whole"), (rates_v, "whole"),
         (before_rows, "whole"), (before_cols, "whole"), (sum_rows, "whole"), (core, "scalar")],
        [(plane, "channels"), (plane, "channels"), ((POS, states * 8, LANES), "whole"),
         ((POS, states * 8, LANES), "whole"), ((states, D), "whole")],
        [size_v, all_rates], 25,
    )
    grad_decay = total_of(grad_decay, rows, cols)
    grad_features, grad_step, grad_write, grad_read = run(
        Unpack(),
        [(features_p, "first"), (steps_p, "first"), (sum_w, "first"), (sum_r, "first")],
        [(packed, "second"), (packed, "second"), (weights, "second"), (weights, "second")],
        [turned],
    )
    weights = (tile_h, states, tile_w)
    return (
        grad_features.reshape(features.shape),
        grad_step.reshape(features.shape),
        grad_write.reshape(weights).swapaxes(1, 2),
        grad_read.reshape(weights).swapaxes(1, 2),
        grad_decay,
    )


def solution(mesh):
    spec = P("row", "col", None)
    sizes = (mesh.shape["row"], mesh.shape["col"])
    return jax.shard_map(
        functools.partial(shards, sizes=sizes),
        mesh=mesh,
        in_specs=(spec, spec, spec, spec, P(), spec),
        out_specs=(spec, spec, spec, spec, P()),
        check_vma=False,
    )
```

```python
import functools

import jax
import jax.numpy as jnp
import numpy as np
from jax import lax
from jax.experimental import pallas as pl
from jax.experimental.pallas import tpu as pltpu
from jax.sharding import PartitionSpec as P

HS, WS, BI, BJ = 8, 16, 4, 4
POS = BI * BJ
LANES = 128
D = 128
STEPS = 4
BLOCK = D // STEPS
F32 = jnp.float32
BF16 = jnp.bfloat16
LOG2E = 1.4426950408889634
LN2 = 0.6931471805599453


@functools.cache
def lane_orders():
    lane = np.arange(LANES)
    hs, ws = lane // WS, lane % WS
    same_w = ws[:, None] == ws[None]
    same_h = hs[:, None] == hs[None]
    out = {
        "above": same_w & (hs[:, None] < hs[None]), "below": same_w & (hs[:, None] > hs[None]),
        "left": same_h & (ws[:, None] < ws[None]), "right": same_h & (ws[:, None] > ws[None]),
    }
    return {k: np.concatenate([v, v], 0).astype(np.float32) for k, v in out.items()}


def lane_places(rows, out):
    at = lax.broadcasted_iota(jnp.int32, (2 * LANES, LANES), 0) % LANES
    lane = lax.broadcasted_iota(jnp.int32, (2 * LANES, LANES), 1)
    segment, edge = (at, lane) if out else (lane, at)
    return edge - (segment % WS if rows else segment // WS)


def edge_start(b, k, rows):
    return (b // 2) * 64 + k * WS if rows else b * 32 + k * HS


def placed(places, start):
    return jnp.where(places == start, 1.0, 0.0).astype(BF16)


def halves(x):
    high = x.astype(BF16)
    low = (x - high.astype(F32)).astype(BF16)
    return high, low


def lane_dot(matrix, *parts):
    parts = [h for x in parts for h in halves(x)]
    return jnp.dot(jnp.concatenate(parts, 1), matrix, preferred_element_type=F32)


def lane_dot_exact(x, matrix):
    high, low = halves(x)
    rest = (x - high.astype(F32) - low.astype(F32)).astype(BF16)
    return jnp.dot(
        jnp.concatenate([high, low], 1), matrix, preferred_element_type=F32
    ) + jnp.dot(rest, matrix[:LANES], preferred_element_type=F32)


def row_of(ref, p, n):
    return jnp.broadcast_to(ref[p, pl.ds(n, 1), :], (8, LANES))


def block_of(b):
    return pl.ds(pl.multiple_of(b * BLOCK, BLOCK), BLOCK)


def half_of(b):
    return pl.ds(pl.multiple_of((b % 2) * BLOCK, BLOCK), BLOCK)


def each_group(b, states, size, body):
    groups = states // size

    def one(at, carry):
        d = pl.ds(pl.multiple_of(b * BLOCK + (at // groups) * 8, 8), 8)
        body([(at % groups) * size + k for k in range(size)], d)
        return carry

    lax.fori_loop(0, (BLOCK // 8) * groups, one, 0)


def send(b, seg, order, leaving, rows):
    states = seg.shape[0]
    at = block_of(b)
    total = None
    places = lane_places(rows, True)
    for k in range(4):
        matrix = jnp.concatenate([placed(places, edge_start(b, k, rows)), order[...]], 1)
        both = lane_dot(matrix, seg[:, k, at].reshape(states * BLOCK, LANES))
        seg[:, k, at] = both[:, LANES:].reshape(states, BLOCK, LANES)
        total = both[:, :LANES] if total is None else total + both[:, :LANES]
    total = total.reshape(states, BLOCK, LANES)
    if rows:
        leaving[:, half_of(b)] += total
    else:
        leaving[...] += total


def take(b, seg, entering, out, rows):
    states = seg.shape[0]
    entering = entering[:, half_of(b)] if rows else entering[...]
    places = lane_places(rows, False)
    matrix = jnp.concatenate([placed(places, edge_start(b, k, rows)) for k in range(4)], 1)
    first = lane_dot(matrix, entering.reshape(states * BLOCK, LANES))
    at = block_of(b)
    for k in range(4):
        out[:, k, at] = seg[:, k, at] + first[:, k * LANES : (k + 1) * LANES].reshape(
            states, BLOCK, LANES
        )


def part_by_core(core, whole, keep, give):
    count = whole.shape[0] // 2
    for n in range(count):
        low, high = whole[n], whole[count + n]
        keep[n] = jnp.where(core[0] == 0, low, high)
        give[n] = jnp.where(core[0] == 0, high, low)


def join_by_core(core, keep, got, whole):
    count = whole.shape[0] // 2
    for n in range(count):
        whole[n] = jnp.where(core[0] == 0, keep[n], got[n])
        whole[count + n] = jnp.where(core[0] == 0, got[n], keep[n])


def gather_plane(ref, i, j):
    return jnp.concatenate([ref[hs, i, pl.ds(j, WS, stride=BJ), :] for hs in range(HS)], 0).T


def gather_states(ref, i, turned, out):
    for hs in range(HS):
        turned[hs] = ref[hs, i].T
    for j in range(BJ):
        out[i * BJ + j] = jnp.concatenate(
            [turned[hs, pl.ds(j, WS, stride=BJ), :] for hs in range(HS)], 0
        ).T


def pack_rates(i, decay_log, rates, rates_v, rates_s):
    lane = lax.broadcasted_iota(jnp.int32, (BLOCK, LANES), 1)
    lane_v = lax.broadcasted_iota(jnp.int32, (2 * BLOCK, LANES), 1)
    rate = (-LOG2E * jnp.exp(decay_log[i])).T
    count = rates.shape[0] // BI
    for k in range(count):
        n = i * count + k
        r = jnp.broadcast_to(rate[:, k : k + 1], (D, LANES))
        rates[n] = r
        part = [r[q * BLOCK : (q + 1) * BLOCK] for q in range(4)]
        rates_v[n] = jnp.where(lane_v < 64, r[: 2 * BLOCK], r[2 * BLOCK :])
        rates_s[n] = jnp.where(
            lane < 64, jnp.where(lane < 32, part[0], part[1]),
            jnp.where(lane < 96, part[2], part[3]),
        )


class AdjointCols:
    def first(self, step, grad, read, decay_log, place, left, right,
              step_p, grad_p, rates, seg, read_p, rates_v, rates_s, own_rates, before_cols,
              sum_cols, sum_rows, sent, turned, leaving):
        sum_cols[...] = jnp.zeros_like(sum_cols)
        leaving[...] = jnp.zeros_like(leaving)
        for i in range(BI):
            pack_rates(i, decay_log, rates, rates_v, rates_s)

    def lead(self, i, step, grad, read, decay_log, place, left, right,
             step_p, grad_p, rates, seg, read_p, rates_v, rates_s, own_rates, before_cols,
             sum_cols, sum_rows, sent, turned, leaving):
        row_total = None
        for j in range(BJ):
            s = gather_plane(step, i, j)
            step_p[i * BJ + j] = s
            grad_p[i * BJ + j] = gather_plane(grad, i, j)
            row_total = s if row_total is None else row_total + s
        gather_states(read, i, turned, read_p)
        before_cols[i] = lane_dot_exact(row_total, left[...])
        places = lane_places(False, True)
        for q in range(STEPS):
            sum_cols[...] += lane_dot_exact(
                row_total[q * BLOCK : (q + 1) * BLOCK], placed(places, edge_start(q, i, False))
            )

    def main(self, b, step, grad, read, decay_log, place, left, right,
             step_p, grad_p, rates, seg, read_p, rates_v, rates_s, own_rates, before_cols,
             sum_cols, sum_rows, sent, turned, leaving):
        states = seg.shape[0]

        def group(ns, d):
            r = [rates[n, d] for n in ns]
            for i in range(BI):
                acc = [None] * len(ns)
                c = before_cols[i, d]
                for j in range(BJ):
                    p = i * BJ + j
                    c = c + step_p[p, d]
                    g = grad_p[p, d]
                    for k, n in enumerate(ns):
                        term = jnp.exp2(c * r[k]) * g * row_of(read_p, p, n)
                        acc[k] = term if acc[k] is None else acc[k] + term
                for k, n in enumerate(ns):
                    seg[n, i, d] = acc[k]

        each_group(b, states, 16, group)
        send(b, seg, right, leaving, False)

    def last(self, step, grad, read, decay_log, place, left, right,
             step_p, grad_p, rates, seg, read_p, rates_v, rates_s, own_rates, before_cols,
             sum_cols, sum_rows, sent, turned, leaving):
        share = own_rates.shape[0]
        for k in range(sent.shape[0]):
            sent[k, 0:share] = leaving[k * share : (k + 1) * share]
            sent[k, share] = sum_cols[...]
        for k in range(share):
            own_rates[k] = rates_s[place[0] * share + k]
        places = lane_places(True, True)
        for r in range(2):
            total = None
            for q in (r, r + 2):
                for j in range(BJ):
                    run = None
                    for i in range(BI):
                        s = step_p[i * BJ + j, q * BLOCK : (q + 1) * BLOCK]
                        run = s if run is None else run + s
                    one = lane_dot_exact(run, placed(places, edge_start(q, j, True)))
                    total = one if total is None else total + one
            sum_rows[r * BLOCK : (r + 1) * BLOCK] = total


class ForwardRows:
    def first(self, feat, step_p, rates, write, rates_v, sum_rows, core, above,
              source_p, seg, write_p, before_rows, keep, give, turned, leaving):
        leaving[...] = jnp.zeros_like(leaving)

    def lead(self, i, feat, step_p, rates, write, rates_v, sum_rows, core, above,
             source_p, seg, write_p, before_rows, keep, give, turned, leaving):
        for j in range(BJ):
            source_p[i * BJ + j] = step_p[i * BJ + j] * gather_plane(feat, i, j)
        gather_states(write, i, turned, write_p)

        @pl.when(i == BI - 1)
        def _():
            for j in range(BJ):
                run = step_p[j]
                for k in range(1, BI):
                    run = run + step_p[k * BJ + j]
                before_rows[j] = lane_dot_exact(run, above[...])

    def main(self, b, feat, step_p, rates, write, rates_v, sum_rows, core, above,
             source_p, seg, write_p, before_rows, keep, give, turned, leaving):
        states = seg.shape[0]

        def group(ns, d):
            r = [-rates[n, d] for n in ns]
            for j in range(BJ):
                acc = [None] * len(ns)
                c = before_rows[j, d]
                for i in range(BI):
                    p = i * BJ + j
                    c = c + step_p[p, d]
                    s = source_p[p, d]
                    for k, n in enumerate(ns):
                        term = jnp.exp2(c * r[k]) * s * row_of(write_p, p, n)
                        acc[k] = term if acc[k] is None else acc[k] + term
                for k, n in enumerate(ns):
                    seg[n, j, d] = acc[k]

        each_group(b, states, 16, group)
        send(b, seg, above, leaving, True)

    def last(self, feat, step_p, rates, write, rates_v, sum_rows, core, above,
             source_p, seg, write_p, before_rows, keep, give, turned, leaving):
        for n in range(leaving.shape[0]):
            leaving[n] = leaving[n] * jnp.exp2(rates_v[n] * sum_rows[...])
        part_by_core(core, leaving, keep, give)


class ForwardCols:
    def first(self, step_p, source_p, rates, seg_rows, keep, got, write_p, rates_s, before_rows,
              before_cols, sum_cols, core, left, start_rows, seg, leaving, entering):
        leaving[...] = jnp.zeros_like(leaving)
        join_by_core(core, keep, got, entering)

    def main(self, b, step_p, source_p, rates, seg_rows, keep, got, write_p, rates_s, before_rows,
             before_cols, sum_cols, core, left, start_rows, seg, leaving, entering):
        states = seg.shape[0]
        take(b, seg_rows, entering, start_rows, True)

        def group(ns, d):
            r = [rates[n, d] for n in ns]
            vert = [[None] * BJ for _ in ns]
            for j in range(BJ):
                before = before_rows[j, d]
                for k, n in enumerate(ns):
                    vert[k][j] = start_rows[n, j, d] * jnp.exp2(r[k] * before)
                    start_rows[n, j, d] = vert[k][j]
            for i in range(BI):
                state = [None] * len(ns)
                after = before_cols[i, d]
                for j in range(BJ):
                    p = i * BJ + j
                    c, s = step_p[p, d], source_p[p, d]
                    after = after + c
                    for k, n in enumerate(ns):
                        decay = jnp.exp2(c * r[k])
                        vert[k][j] = decay * vert[k][j] + s * row_of(write_p, p, n)
                        state[k] = vert[k][j] if j == 0 else decay * state[k] + vert[k][j]
                for k, n in enumerate(ns):
                    seg[n, i, d] = state[k] * jnp.exp2(-r[k] * after)

        each_group(b, states, 8, group)
        send(b, seg, left, leaving, False)

    def last(self, step_p, source_p, rates, seg_rows, keep, got, write_p, rates_s, before_rows,
             before_cols, sum_cols, core, left, start_rows, seg, leaving, entering):
        for n in range(leaving.shape[0]):
            leaving[n] = leaving[n] * jnp.exp2(rates_s[n] * sum_cols[...])


class AdjointRows:
    def first(self, step_p, grad_p, rates, seg_cols, entering, read_p, rates_s, before_rows,
              before_cols, sum_cols, core, below, start_cols, seg, keep, give,
              scaled, leaving):
        leaving[...] = jnp.zeros_like(leaving)
        for n in range(scaled.shape[0]):
            scaled[n] = entering[n] * jnp.exp2(rates_s[n] * sum_cols[...])

    def main(self, b, step_p, grad_p, rates, seg_cols, entering, read_p, rates_s, before_rows,
             before_cols, sum_cols, core, below, start_cols, seg, keep, give,
             scaled, leaving):
        states = seg.shape[0]
        take(b, seg_cols, scaled, start_cols, False)

        def group(ns, d):
            r = [rates[n, d] for n in ns]
            passed_v = [[None] * BJ for _ in ns]
            for i in reversed(range(BI)):
                after = before_cols[i, d]
                for j in range(BJ):
                    after = after + step_p[i * BJ + j, d]
                passed = []
                for k, n in enumerate(ns):
                    passed.append(start_cols[n, i, d] * jnp.exp2(-r[k] * after))
                    start_cols[n, i, d] = passed[k]
                for j in reversed(range(BJ)):
                    p = i * BJ + j
                    c, g = step_p[p, d], grad_p[p, d]
                    for k, n in enumerate(ns):
                        decay = jnp.exp2(c * r[k])
                        adjoint = g * row_of(read_p, p, n) + passed[k]
                        passed[k] = decay * adjoint
                        if i == BI - 1:
                            passed_v[k][j] = passed[k]
                        else:
                            passed_v[k][j] = decay * (adjoint + passed_v[k][j])
            for j in range(BJ):
                before = before_rows[j, d]
                for k, n in enumerate(ns):
                    seg[n, j, d] = passed_v[k][j] * jnp.exp2(r[k] * before)

        each_group(b, states, 8, group)
        send(b, seg, below, leaving, True)

    def last(self, step_p, grad_p, rates, seg_cols, entering, read_p, rates_s, before_rows,
             before_cols, sum_cols, core, below, start_cols, seg, keep, give,
             scaled, leaving):
        part_by_core(core, leaving, keep, give)


class Final:
    def first(self, step_p, source_p, grad_p, rates, start_rows, start_cols, seg_s, seg_v,
              enter_s, keep, got, write_p, read_p, rates_v, before_rows, before_cols, sum_rows,
              core, features_p, steps_p, sum_w, sum_r, grad_decay,
              entering, decay_term):
        join_by_core(core, keep, got, entering)
        for n in range(entering.shape[0]):
            entering[n] = entering[n] * jnp.exp2(rates_v[n] * sum_rows[...])
        sum_w[...] = jnp.zeros_like(sum_w)
        sum_r[...] = jnp.zeros_like(sum_r)

    def main(self, b, step_p, source_p, grad_p, rates, start_rows, start_cols, seg_s, seg_v,
             enter_s, keep, got, write_p, read_p, rates_v, before_rows, before_cols, sum_rows,
             core, features_p, steps_p, sum_w, sum_r, grad_decay,
             entering, decay_term):
        states = rates.shape[0]
        take(b, seg_s, enter_s, seg_s, False)
        take(b, seg_v, entering, seg_v, True)
        at = block_of(b)
        features_p[:, at] = jnp.zeros((POS, BLOCK, LANES), F32)
        steps_p[:, at] = jnp.zeros((POS, BLOCK, LANES), F32)

        def group(ns, d):
            r = [rates[n, d] for n in ns]
            vert = [[start_rows[n, j, d] for j in range(BJ)] for n in ns]
            from_v, from_s = [{} for _ in ns], [{} for _ in ns]
            exps = [{} for _ in ns]
            for i in range(BI):
                before = before_cols[i, d]
                state = [seg_s[n, i, d] * jnp.exp2(r[k] * before) for k, n in enumerate(ns)]
                for j in range(BJ):
                    p = i * BJ + j
                    c, s, g = step_p[p, d], source_p[p, d], grad_p[p, d]
                    for k, n in enumerate(ns):
                        m = c * r[k]
                        decay = jnp.exp2(m)
                        dv = decay * vert[k][j]
                        vert[k][j] = dv + s * row_of(write_p, p, n)
                        ds = decay * state[k]
                        state[k] = ds + vert[k][j]
                        sum_r[p, pl.ds(n * 8, 8)] += state[k] * g
                        from_v[k][p] = dv
                        from_s[k][p] = ds
                        exps[k][p] = m
            passed_v = [[None] * BJ for _ in ns]
            for j in range(BJ):
                after = before_rows[j, d]
                for i in range(BI):
                    after = after + step_p[i * BJ + j, d]
                for k, n in enumerate(ns):
                    passed_v[k][j] = seg_v[n, j, d] * jnp.exp2(-r[k] * after)
            total = [None for _ in ns]
            for i in reversed(range(BI)):
                passed = [start_cols[n, i, d] for n in ns]
                for j in reversed(range(BJ)):
                    p = i * BJ + j
                    s, g = source_p[p, d], grad_p[p, d]
                    sum_q, sum_t = None, None
                    for k, n in enumerate(ns):
                        adjoint = g * row_of(read_p, p, n) + passed[k]
                        m = exps[k][p]
                        decay = jnp.exp2(m)
                        passed[k] = decay * adjoint
                        adjoint_v = adjoint + passed_v[k][j]
                        passed_v[k][j] = decay * adjoint_v
                        q = (adjoint * from_s[k][p] + adjoint_v * from_v[k][p]) * m
                        total[k] = q if total[k] is None else total[k] + q
                        t = adjoint_v * row_of(write_p, p, n)
                        sum_q = q if sum_q is None else sum_q + q
                        sum_t = t if sum_t is None else sum_t + t
                        sum_w[p, pl.ds(n * 8, 8)] += adjoint_v * s
                    steps_p[p, d] += sum_q
                    features_p[p, d] += sum_t
            for k, n in enumerate(ns):
                decay_term[n, d] = total[k]

        each_group(b, states, 8, group)
        for p in range(POS):
            t, s = features_p[p, at], step_p[p, at]
            features_p[p, at] = s * t
            steps_p[p, at] = (source_p[p, at] * t + steps_p[p, at] * LN2) / s

    def last(self, step_p, source_p, grad_p, rates, start_rows, start_cols, seg_s, seg_v,
             enter_s, keep, got, write_p, read_p, rates_v, before_rows, before_cols, sum_rows,
             core, features_p, steps_p, sum_w, sum_r, grad_decay,
             entering, decay_term):
        for n in range(rates.shape[0]):
            out = lax.dot_general(
                jnp.ones((8, 2 * LANES), BF16), jnp.concatenate(halves(decay_term[n]), 1),
                (((1,), (1,)), ((), ())), preferred_element_type=F32,
            )
            grad_decay[pl.ds(n, 1)] = out[0:1] * LN2


class Unpack:
    def lead(self, i, features_p, steps_p, sum_w, sum_r, features, steps, writes, reads, turned):
        for j in range(BJ):
            for values, out in ((features_p, features), (steps_p, steps)):
                back = values[i * BJ + j].T
                for hs in range(HS):
                    out[hs, i, pl.ds(j, WS, stride=BJ), :] = back[hs * WS : hs * WS + WS]
        states = writes.shape[2]
        for values, out in ((sum_w, writes), (sum_r, reads)):
            for j in range(BJ):
                back = sum(values[i * BJ + j, pl.ds(k, states, stride=8), :] for k in range(8)).T
                for hs in range(HS):
                    turned[hs, pl.ds(j, WS, stride=BJ), :] = back[hs * WS : hs * WS + WS]
            for hs in range(HS):
                out[hs, i] = turned[hs].T


def prefix_kernel(held, sums, rates, out, *, reverse):
    size, share = out.shape[:2]
    at = sums.shape[1] - 1
    order = list(reversed(range(size))) if reverse else list(range(size))
    for n in range(share):
        before = jnp.zeros(out.shape[2:], F32)
        for k in order:
            out[k, n] = before
            before = jnp.exp2(rates[n] * sums[k, at]) * before + held[k, n]


def cut(ref, kind, k):
    if kind == "channels":
        index = (slice(None),) * (len(ref.shape) - 2) + (block_of(k),)
        return ref.at[index]
    if kind == "second":
        return ref.at[:, k]
    size = ref.shape[0] // BI
    return ref.at[pl.ds(k * size, size)]


def run(stage, ins, outs, scratch=(), micros=5):
    in_kinds, out_kinds = [k for _, k in ins], [k for _, k in outs]
    shapes = [a.shape for a, _ in ins] + [s for s, _ in outs]
    types = [a.dtype for a, _ in ins] + [F32 for _ in outs]
    kinds = in_kinds + out_kinds
    phase = {"whole": 0, "second": 1, "first": 1, "channels": 2}
    copied = [at for at, k in enumerate(kinds) if k in phase]
    count = len(ins)

    def kernel(*refs):
        given = list(refs[: len(kinds)])
        rest = refs[len(kinds) :]
        buffers, sems = rest[: len(copied)], rest[len(copied)]
        extra = rest[len(copied) + 1 :]
        views = list(given)
        into, out_of = [[], [], []], [[], [], []]
        for slot, at in enumerate(copied):
            views[at] = buffers[slot]

            def copy(k, slot=slot, at=at):
                far, near = given[at], buffers[slot]
                if kinds[at] != "whole":
                    far, near = cut(far, kinds[at], k), cut(near, kinds[at], k)
                pair = (far, near) if at < count else (near, far)
                return pltpu.make_async_copy(*pair, sems.at[slot, k])

            (into if at < count else out_of)[phase[kinds[at]]].append(copy)

        def part(which, name):
            def one(k, carry):
                for copy in into[which]:
                    copy(k).wait()
                getattr(stage, name)(k, *views, *extra)
                for copy in out_of[which]:
                    copy(k).start()
                return carry

            lax.fori_loop(0, STEPS, one, 0)

        for which in range(3):
            for k in range(STEPS if which else 1):
                for copy in into[which]:
                    copy(k).start()
        for copy in into[0]:
            copy(0).wait()
        if hasattr(stage, "first"):
            stage.first(*views, *extra)
        if hasattr(stage, "lead"):
            part(1, "lead")
        if hasattr(stage, "main"):
            part(2, "main")
        if hasattr(stage, "last"):
            stage.last(*views, *extra)
        for copy in out_of[0]:
            copy(0).start()
        for which in range(3):
            for k in range(STEPS if which else 1):
                for copy in out_of[which]:
                    copy(k).wait()

    def spec(kind):
        if kind == "small":
            return pl.BlockSpec(memory_space=pltpu.VMEM)
        if kind == "scalar":
            return pl.BlockSpec(memory_space=pltpu.SMEM)
        return pl.BlockSpec(memory_space=pl.ANY)

    return pl.pallas_call(
        kernel,
        out_shape=[jax.ShapeDtypeStruct(s, F32) for s, _ in outs],
        in_specs=[spec(k) for k in in_kinds],
        out_specs=[spec(k) for k in out_kinds],
        scratch_shapes=[pltpu.VMEM(shapes[at], types[at]) for at in copied]
        + [pltpu.SemaphoreType.DMA((len(copied), STEPS))]
        + [pltpu.VMEM(s, F32) for s in scratch],
        compiler_params=pltpu.CompilerParams(vmem_limit_bytes=60 << 20),
        cost_estimate=pl.CostEstimate(
            flops=0, bytes_accessed=int(micros * 3.3e6), transcendentals=0
        ),
    )(*[a for a, _ in ins])


def swap_cores(x, size):
    return lax.ppermute(x, "row", [(k, k ^ 1) for k in range(size)])


def tied(*arrays):
    return lax.optimization_barrier(arrays)


def row_total(keep, give, sums, other_sums, rates, size, reverse):
    count = keep.shape[0]
    core = lax.axis_index("row") % 2
    theirs = swap_cores(give, size)
    rate = lax.dynamic_slice_in_dim(rates, core * count, count, 0)
    first = core == (1 if reverse else 0)
    near = jnp.where(first, keep, theirs)
    far = jnp.where(first, theirs, keep)
    near_sum = jnp.where(first, sums, other_sums)
    far_sum = jnp.where(first, other_sums, sums)
    total = far + jnp.exp2(rate * far_sum) * near
    return total, near, near_sum, far_sum, rate


def row_carry(total, near, near_sum, far_sum, rate, beside, size, reverse):
    core = lax.axis_index("row") % 2
    first = core == (1 if reverse else 0)
    sign = -2 if reverse else 2

    def shift(x, by):
        return lax.ppermute(
            x, "row", [(k, k + by) for k in range(size) if 0 <= k + by < size]
        )

    entering = shift(total, sign)
    if size > 4:
        span = shift(near_sum + far_sum, sign)
        by = sign
        while abs(by) < size - 2:
            entering = entering + jnp.exp2(rate * span) * shift(entering, by)
            span = span + shift(span, by)
            by *= 2
    entering, _ = tied(entering, beside)
    to_far = near + jnp.exp2(rate * near_sum) * entering
    keep = jnp.where(first, entering, to_far)
    give = jnp.where(first, to_far, entering)
    return keep, swap_cores(give, size)


def col_gather(sent):
    return lax.all_to_all(sent, "col", 0, 0)


def col_carry(held, sums, rates, reverse):
    size, share = held.shape[0], rates.shape[0]
    vmem = pl.BlockSpec(memory_space=pltpu.VMEM)
    return pl.pallas_call(
        functools.partial(prefix_kernel, reverse=reverse),
        out_shape=jax.ShapeDtypeStruct((size, share) + held.shape[2:], F32),
        in_specs=[vmem] * 3,
        out_specs=vmem,
        compiler_params=pltpu.CompilerParams(vmem_limit_bytes=4 << 20),
    )(held, sums, rates)


def col_return(carries):
    back = lax.all_to_all(carries, "col", 0, 0)
    return back.reshape((-1,) + carries.shape[2:])


def total_of(x, rows, cols):
    terms = [x] + [
        lax.ppermute(x, "row", [(k, k ^ by) for k in range(rows)]) for by in range(1, rows)
    ]
    while len(terms) > 1:
        terms = [a + b for a, b in zip(terms[::2], terms[1::2])]
    parts = lax.all_to_all(jnp.broadcast_to(terms[0][None], (cols,) + x.shape), "col", 0, 0)
    return jnp.sum(parts, 0)


def shards(features, step_size, write_weights, read_weights, decay_log, out_grad, sizes):
    rows, cols = sizes
    states = decay_log.shape[0]
    share = states // cols
    tile_h, tile_w = features.shape[:2]
    orders = {k: jnp.asarray(v, BF16) for k, v in lane_orders().items()}
    plane, quad = (POS, D, LANES), (4, D, LANES)
    seg = (states, 4, D, LANES)
    all_rates = (states, D, LANES)
    small = (POS, states, LANES)
    packed = (HS, BI, tile_w, D)
    weights = (HS, BI, states, tile_w)
    turned = (HS, tile_w, states)
    size_v, size_s = (states, D // 2, LANES), (states, D // 4, LANES)
    half_v = (states // 2,) + size_v[1:]
    core = (lax.axis_index("row") % 2).astype(jnp.int32).reshape(1)
    place = lax.axis_index("col").astype(jnp.int32).reshape(1)

    (step_p, grad_p, rates, seg_cols, read_p, rates_v, rates_s, own_rates, before_cols, sum_cols,
     sum_rows, sent) = run(
        AdjointCols(),
        [(step_size.reshape(packed), "second"), (out_grad.reshape(packed), "second"),
         (read_weights.swapaxes(1, 2).reshape(weights), "second"),
         (decay_log.reshape(BI, states // BI, D), "small"), (place, "scalar"),
         (orders["left"], "whole"), (orders["right"], "whole")],
        [(plane, "first"), (plane, "first"), (all_rates, "first"), (seg, "channels"),
         (small, "whole"), (size_v, "whole"), (size_s, "whole"), ((share,) + size_s[1:], "whole"),
         (quad, "whole"), (size_s[1:], "whole"), (size_v[1:], "whole"),
         ((cols, share + 1) + size_s[1:], "whole")],
        [turned, size_s],
    )
    held = col_gather(sent)
    other_rows = swap_cores(sum_rows, rows)
    step_p, _ = tied(step_p, sent)
    source_p, seg_rows, write_p, before_rows, keep, give = run(
        ForwardRows(),
        [(features.reshape(packed), "second"), (step_p, "first"), (rates, "channels"),
         (write_weights.swapaxes(1, 2).reshape(weights), "second"), (rates_v, "whole"),
         (sum_rows, "whole"), (core, "scalar"), (orders["above"], "whole")],
        [(plane, "first"), (seg, "channels"), (small, "whole"), (quad, "whole"),
         (half_v, "whole"), (half_v, "whole")],
        [turned, size_v],
    )
    total = row_total(keep, give, sum_rows, other_rows, rates_v, rows, False)
    held, first = tied(held, total[0])
    col_sums = held
    carries = col_carry(held, held, own_rates, True)
    enter_cols = col_return(carries)
    keep, got = row_carry(first, *total[1:], carries, rows, False)
    start_rows, seg_s, leave_s = run(
        ForwardCols(),
        [(step_p, "channels"), (source_p, "channels"), (rates, "channels"),
         (seg_rows, "channels"), (keep, "whole"), (got, "whole"), (write_p, "whole"),
         (rates_s, "whole"), (before_rows, "whole"), (before_cols, "whole"),
         (sum_cols, "whole"), (core, "scalar"), (orders["left"], "whole")],
        [(seg, "channels"), (seg, "channels"), (size_s, "whole")], [size_v], 10,
    )
    held = col_gather(leave_s.reshape((cols, share) + size_s[1:]))
    enter_cols, _ = tied(enter_cols, leave_s)
    start_cols, seg_v, keep, give = run(
        AdjointRows(),
        [(step_p, "channels"), (grad_p, "channels"), (rates, "channels"),
         (seg_cols, "channels"), (enter_cols, "whole"), (read_p, "whole"), (rates_s, "whole"),
         (before_rows, "whole"), (before_cols, "whole"), (sum_cols, "whole"), (core, "scalar"),
         (orders["below"], "whole")],
        [(seg, "channels"), (seg, "channels"), (half_v, "whole"), (half_v, "whole")],
        [size_s, size_v], 10,
    )
    held, give = tied(held, give)
    total = row_total(keep, give, sum_rows, other_rows, rates_v, rows, True)
    held, first = tied(held, total[0])
    carries = col_carry(held, col_sums, own_rates, False)
    enter_s = col_return(carries)
    keep, got = row_carry(first, *total[1:], carries, rows, True)
    features_p, steps_p, sum_w, sum_r, grad_decay = run(
        Final(),
        [(step_p, "channels"), (source_p, "channels"), (grad_p, "channels"),
         (rates, "channels"), (start_rows, "channels"), (start_cols, "channels"),
         (seg_s, "channels"), (seg_v, "channels"), (enter_s, "whole"), (keep, "whole"),
         (got, "whole"), (write_p, "whole"), (read_p, "whole"), (rates_v, "whole"),
         (before_rows, "whole"), (before_cols, "whole"), (sum_rows, "whole"), (core, "scalar")],
        [(plane, "channels"), (plane, "channels"), ((POS, states * 8, LANES), "whole"),
         ((POS, states * 8, LANES), "whole"), ((states, D), "whole")],
        [size_v, all_rates], 25,
    )
    grad_decay = total_of(grad_decay, rows, cols)
    grad_features, grad_step, grad_write, grad_read = run(
        Unpack(),
        [(features_p, "first"), (steps_p, "first"), (sum_w, "first"), (sum_r, "first")],
        [(packed, "second"), (packed, "second"), (weights, "second"), (weights, "second")],
        [turned],
    )
    weights = (tile_h, states, tile_w)
    return (
        grad_features.reshape(features.shape),
        grad_step.reshape(features.shape),
        grad_write.reshape(weights).swapaxes(1, 2),
        grad_read.reshape(weights).swapaxes(1, 2),
        grad_decay,
    )


def solution(mesh):
    spec = P("row", "col", None)
    sizes = (mesh.shape["row"], mesh.shape["col"])
    return jax.shard_map(
        functools.partial(shards, sizes=sizes),
        mesh=mesh,
        in_specs=(spec, spec, spec, spec, P(), spec),
        out_specs=(spec, spec, spec, spec, P()),
        check_vma=False,
    )
```

```python
import functools

import jax
import jax.numpy as jnp
import numpy as np
from jax import lax
from jax.experimental import pallas as pl
from jax.experimental.pallas import tpu as pltpu
from jax.sharding import PartitionSpec as P

HS, WS, BI, BJ = 8, 16, 4, 4
POS = BI * BJ
LANES = 128
D = 128
STEPS = 4
BLOCK = D // STEPS
F32 = jnp.float32
BF16 = jnp.bfloat16
LOG2E = 1.4426950408889634
LN2 = 0.6931471805599453


@functools.cache
def lane_orders():
    lane = np.arange(LANES)
    hs, ws = lane // WS, lane % WS
    same_w = ws[:, None] == ws[None]
    same_h = hs[:, None] == hs[None]
    out = {
        "above": same_w & (hs[:, None] < hs[None]), "below": same_w & (hs[:, None] > hs[None]),
        "left": same_h & (ws[:, None] < ws[None]), "right": same_h & (ws[:, None] > ws[None]),
    }
    return {k: np.concatenate([v, v], 0).astype(np.float32) for k, v in out.items()}


def lane_places(rows, out):
    at = lax.broadcasted_iota(jnp.int32, (2 * LANES, LANES), 0) % LANES
    lane = lax.broadcasted_iota(jnp.int32, (2 * LANES, LANES), 1)
    segment, edge = (at, lane) if out else (lane, at)
    return edge - (segment % WS if rows else segment // WS)


def edge_start(b, k, rows):
    return (b // 2) * 64 + k * WS if rows else b * 32 + k * HS


def placed(places, start):
    return jnp.where(places == start, 1.0, 0.0).astype(BF16)


def halves(x):
    high = x.astype(BF16)
    low = (x - high.astype(F32)).astype(BF16)
    return high, low


def lane_dot(matrix, *parts):
    parts = [h for x in parts for h in halves(x)]
    return jnp.dot(jnp.concatenate(parts, 1), matrix, preferred_element_type=F32)


def lane_dot_exact(x, matrix):
    high, low = halves(x)
    rest = (x - high.astype(F32) - low.astype(F32)).astype(BF16)
    return jnp.dot(
        jnp.concatenate([high, low], 1), matrix, preferred_element_type=F32
    ) + jnp.dot(rest, matrix[:LANES], preferred_element_type=F32)


def row_of(ref, p, n):
    return jnp.broadcast_to(ref[p, pl.ds(n, 1), :], (8, LANES))


def block_of(b):
    return pl.ds(pl.multiple_of(b * BLOCK, BLOCK), BLOCK)


def half_of(b):
    return pl.ds(pl.multiple_of((b % 2) * BLOCK, BLOCK), BLOCK)


def each_group(b, states, size, body):
    groups = states // size

    def one(at, carry):
        d = pl.ds(pl.multiple_of(b * BLOCK + (at // groups) * 8, 8), 8)
        body([(at % groups) * size + k for k in range(size)], d)
        return carry

    lax.fori_loop(0, (BLOCK // 8) * groups, one, 0)


def send(b, seg, order, leaving, rows):
    states = seg.shape[0]
    at = block_of(b)
    total = None
    places = lane_places(rows, True)
    for k in range(4):
        matrix = jnp.concatenate([placed(places, edge_start(b, k, rows)), order[...]], 1)
        both = lane_dot(matrix, seg[:, k, at].reshape(states * BLOCK, LANES))
        seg[:, k, at] = both[:, LANES:].reshape(states, BLOCK, LANES)
        total = both[:, :LANES] if total is None else total + both[:, :LANES]
    total = total.reshape(states, BLOCK, LANES)
    if rows:
        leaving[:, half_of(b)] += total
    else:
        leaving[...] += total


def take(b, seg, entering, out, rows):
    states = seg.shape[0]
    entering = entering[:, half_of(b)] if rows else entering[...]
    places = lane_places(rows, False)
    matrix = jnp.concatenate([placed(places, edge_start(b, k, rows)) for k in range(4)], 1)
    first = lane_dot(matrix, entering.reshape(states * BLOCK, LANES))
    at = block_of(b)
    for k in range(4):
        out[:, k, at] = seg[:, k, at] + first[:, k * LANES : (k + 1) * LANES].reshape(
            states, BLOCK, LANES
        )


def part_by_core(core, whole, keep, give):
    count = whole.shape[0] // 2
    for n in range(count):
        low, high = whole[n], whole[count + n]
        keep[n] = jnp.where(core[0] == 0, low, high)
        give[n] = jnp.where(core[0] == 0, high, low)


def join_by_core(core, keep, got, whole):
    count = whole.shape[0] // 2
    for n in range(count):
        whole[n] = jnp.where(core[0] == 0, keep[n], got[n])
        whole[count + n] = jnp.where(core[0] == 0, got[n], keep[n])


def gather_plane(ref, i, j):
    return jnp.concatenate([ref[hs, i, pl.ds(j, WS, stride=BJ), :] for hs in range(HS)], 0).T


def gather_states(ref, i, turned, out):
    for hs in range(HS):
        turned[hs] = ref[hs, i].T
    for j in range(BJ):
        out[i * BJ + j] = jnp.concatenate(
            [turned[hs, pl.ds(j, WS, stride=BJ), :] for hs in range(HS)], 0
        ).T


def pack_rates(i, decay_log, rates, rates_v, rates_s):
    lane = lax.broadcasted_iota(jnp.int32, (BLOCK, LANES), 1)
    lane_v = lax.broadcasted_iota(jnp.int32, (2 * BLOCK, LANES), 1)
    rate = (-LOG2E * jnp.exp(decay_log[i])).T
    count = rates.shape[0] // BI
    for k in range(count):
        n = i * count + k
        r = jnp.broadcast_to(rate[:, k : k + 1], (D, LANES))
        rates[n] = r
        part = [r[q * BLOCK : (q + 1) * BLOCK] for q in range(4)]
        rates_v[n] = jnp.where(lane_v < 64, r[: 2 * BLOCK], r[2 * BLOCK :])
        rates_s[n] = jnp.where(
            lane < 64, jnp.where(lane < 32, part[0], part[1]),
            jnp.where(lane < 96, part[2], part[3]),
        )


class AdjointCols:
    def first(self, step, grad, read, decay_log, place, left, right,
              step_p, grad_p, rates, seg, read_p, rates_v, rates_s, own_rates, before_cols,
              sum_cols, sum_rows, sent, turned, leaving):
        sum_cols[...] = jnp.zeros_like(sum_cols)
        leaving[...] = jnp.zeros_like(leaving)
        for i in range(BI):
            pack_rates(i, decay_log, rates, rates_v, rates_s)

    def lead(self, i, step, grad, read, decay_log, place, left, right,
             step_p, grad_p, rates, seg, read_p, rates_v, rates_s, own_rates, before_cols,
             sum_cols, sum_rows, sent, turned, leaving):
        row_total = None
        for j in range(BJ):
            s = gather_plane(step, i, j)
            step_p[i * BJ + j] = s
            grad_p[i * BJ + j] = gather_plane(grad, i, j)
            row_total = s if row_total is None else row_total + s
        gather_states(read, i, turned, read_p)
        before_cols[i] = lane_dot_exact(row_total, left[...])
        places = lane_places(False, True)
        for q in range(STEPS):
            sum_cols[...] += lane_dot_exact(
                row_total[q * BLOCK : (q + 1) * BLOCK], placed(places, edge_start(q, i, False))
            )

    def main(self, b, step, grad, read, decay_log, place, left, right,
             step_p, grad_p, rates, seg, read_p, rates_v, rates_s, own_rates, before_cols,
             sum_cols, sum_rows, sent, turned, leaving):
        states = seg.shape[0]

        def group(ns, d):
            r = [rates[n, d] for n in ns]
            for i in range(BI):
                acc = [None] * len(ns)
                c = before_cols[i, d]
                for j in range(BJ):
                    p = i * BJ + j
                    c = c + step_p[p, d]
                    g = grad_p[p, d]
                    for k, n in enumerate(ns):
                        term = jnp.exp2(c * r[k]) * g * row_of(read_p, p, n)
                        acc[k] = term if acc[k] is None else acc[k] + term
                for k, n in enumerate(ns):
                    seg[n, i, d] = acc[k]

        each_group(b, states, 16, group)
        send(b, seg, right, leaving, False)

    def last(self, step, grad, read, decay_log, place, left, right,
             step_p, grad_p, rates, seg, read_p, rates_v, rates_s, own_rates, before_cols,
             sum_cols, sum_rows, sent, turned, leaving):
        share = own_rates.shape[0]
        for k in range(sent.shape[0]):
            sent[k, 0:share] = leaving[k * share : (k + 1) * share]
            sent[k, share] = sum_cols[...]
        for k in range(share):
            own_rates[k] = rates_s[place[0] * share + k]
        places = lane_places(True, True)
        for r in range(2):
            total = None
            for q in (r, r + 2):
                for j in range(BJ):
                    run = None
                    for i in range(BI):
                        s = step_p[i * BJ + j, q * BLOCK : (q + 1) * BLOCK]
                        run = s if run is None else run + s
                    one = lane_dot_exact(run, placed(places, edge_start(q, j, True)))
                    total = one if total is None else total + one
            sum_rows[r * BLOCK : (r + 1) * BLOCK] = total


class ForwardRows:
    def first(self, feat, step_p, rates, write, rates_v, sum_rows, core, above,
              source_p, seg, write_p, before_rows, keep, give, turned, leaving):
        leaving[...] = jnp.zeros_like(leaving)

    def lead(self, i, feat, step_p, rates, write, rates_v, sum_rows, core, above,
             source_p, seg, write_p, before_rows, keep, give, turned, leaving):
        for j in range(BJ):
            source_p[i * BJ + j] = step_p[i * BJ + j] * gather_plane(feat, i, j)
        gather_states(write, i, turned, write_p)

        @pl.when(i == BI - 1)
        def _():
            for j in range(BJ):
                run = step_p[j]
                for k in range(1, BI):
                    run = run + step_p[k * BJ + j]
                before_rows[j] = lane_dot_exact(run, above[...])

    def main(self, b, feat, step_p, rates, write, rates_v, sum_rows, core, above,
             source_p, seg, write_p, before_rows, keep, give, turned, leaving):
        states = seg.shape[0]

        def group(ns, d):
            r = [-rates[n, d] for n in ns]
            for j in range(BJ):
                acc = [None] * len(ns)
                c = before_rows[j, d]
                for i in range(BI):
                    p = i * BJ + j
                    c = c + step_p[p, d]
                    s = source_p[p, d]
                    for k, n in enumerate(ns):
                        term = jnp.exp2(c * r[k]) * s * row_of(write_p, p, n)
                        acc[k] = term if acc[k] is None else acc[k] + term
                for k, n in enumerate(ns):
                    seg[n, j, d] = acc[k]

        each_group(b, states, 16, group)
        send(b, seg, above, leaving, True)

    def last(self, feat, step_p, rates, write, rates_v, sum_rows, core, above,
             source_p, seg, write_p, before_rows, keep, give, turned, leaving):
        for n in range(leaving.shape[0]):
            leaving[n] = leaving[n] * jnp.exp2(rates_v[n] * sum_rows[...])
        part_by_core(core, leaving, keep, give)


class ForwardCols:
    def first(self, step_p, source_p, rates, seg_rows, keep, got, write_p, rates_s, before_rows,
              before_cols, sum_cols, core, left, start_rows, seg, leaving, entering):
        leaving[...] = jnp.zeros_like(leaving)
        join_by_core(core, keep, got, entering)

    def main(self, b, step_p, source_p, rates, seg_rows, keep, got, write_p, rates_s, before_rows,
             before_cols, sum_cols, core, left, start_rows, seg, leaving, entering):
        states = seg.shape[0]
        take(b, seg_rows, entering, start_rows, True)

        def group(ns, d):
            r = [rates[n, d] for n in ns]
            vert = [[None] * BJ for _ in ns]
            for j in range(BJ):
                before = before_rows[j, d]
                for k, n in enumerate(ns):
                    vert[k][j] = start_rows[n, j, d] * jnp.exp2(r[k] * before)
                    start_rows[n, j, d] = vert[k][j]
            for i in range(BI):
                state = [None] * len(ns)
                after = before_cols[i, d]
                for j in range(BJ):
                    p = i * BJ + j
                    c, s = step_p[p, d], source_p[p, d]
                    after = after + c
                    for k, n in enumerate(ns):
                        decay = jnp.exp2(c * r[k])
                        vert[k][j] = decay * vert[k][j] + s * row_of(write_p, p, n)
                        state[k] = vert[k][j] if j == 0 else decay * state[k] + vert[k][j]
                for k, n in enumerate(ns):
                    seg[n, i, d] = state[k] * jnp.exp2(-r[k] * after)

        each_group(b, states, 8, group)

    def after(self, b, step_p, source_p, rates, seg_rows, keep, got, write_p, rates_s, before_rows,
             before_cols, sum_cols, core, left, start_rows, seg, leaving, entering):
        send(b, seg, left, leaving, False)

    def last(self, step_p, source_p, rates, seg_rows, keep, got, write_p, rates_s, before_rows,
             before_cols, sum_cols, core, left, start_rows, seg, leaving, entering):
        for n in range(leaving.shape[0]):
            leaving[n] = leaving[n] * jnp.exp2(rates_s[n] * sum_cols[...])


class AdjointRows:
    def first(self, step_p, grad_p, rates, seg_cols, entering, read_p, rates_s, before_rows,
              before_cols, sum_cols, core, below, start_cols, seg, keep, give,
              scaled, leaving):
        leaving[...] = jnp.zeros_like(leaving)
        for n in range(scaled.shape[0]):
            scaled[n] = entering[n] * jnp.exp2(rates_s[n] * sum_cols[...])

    def main(self, b, step_p, grad_p, rates, seg_cols, entering, read_p, rates_s, before_rows,
             before_cols, sum_cols, core, below, start_cols, seg, keep, give,
             scaled, leaving):
        states = seg.shape[0]
        take(b, seg_cols, scaled, start_cols, False)

        def group(ns, d):
            r = [rates[n, d] for n in ns]
            passed_v = [[None] * BJ for _ in ns]
            for i in reversed(range(BI)):
                after = before_cols[i, d]
                for j in range(BJ):
                    after = after + step_p[i * BJ + j, d]
                passed = []
                for k, n in enumerate(ns):
                    passed.append(start_cols[n, i, d] * jnp.exp2(-r[k] * after))
                    start_cols[n, i, d] = passed[k]
                for j in reversed(range(BJ)):
                    p = i * BJ + j
                    c, g = step_p[p, d], grad_p[p, d]
                    for k, n in enumerate(ns):
                        decay = jnp.exp2(c * r[k])
                        adjoint = g * row_of(read_p, p, n) + passed[k]
                        passed[k] = decay * adjoint
                        if i == BI - 1:
                            passed_v[k][j] = passed[k]
                        else:
                            passed_v[k][j] = decay * (adjoint + passed_v[k][j])
            for j in range(BJ):
                before = before_rows[j, d]
                for k, n in enumerate(ns):
                    seg[n, j, d] = passed_v[k][j] * jnp.exp2(r[k] * before)

        each_group(b, states, 8, group)

    def after(self, b, step_p, grad_p, rates, seg_cols, entering, read_p, rates_s, before_rows,
             before_cols, sum_cols, core, below, start_cols, seg, keep, give,
             scaled, leaving):
        send(b, seg, below, leaving, True)

    def last(self, step_p, grad_p, rates, seg_cols, entering, read_p, rates_s, before_rows,
             before_cols, sum_cols, core, below, start_cols, seg, keep, give,
             scaled, leaving):
        part_by_core(core, leaving, keep, give)


class Final:
    def first(self, step_p, source_p, grad_p, rates, start_rows, start_cols, seg_s, seg_v,
              enter_s, keep, got, write_p, read_p, rates_v, before_rows, before_cols, sum_rows,
              core, features_p, steps_p, sum_w, sum_r, grad_decay,
              entering, decay_term):
        join_by_core(core, keep, got, entering)
        for n in range(entering.shape[0]):
            entering[n] = entering[n] * jnp.exp2(rates_v[n] * sum_rows[...])
        sum_w[...] = jnp.zeros_like(sum_w)
        sum_r[...] = jnp.zeros_like(sum_r)

    def main(self, b, step_p, source_p, grad_p, rates, start_rows, start_cols, seg_s, seg_v,
             enter_s, keep, got, write_p, read_p, rates_v, before_rows, before_cols, sum_rows,
             core, features_p, steps_p, sum_w, sum_r, grad_decay,
             entering, decay_term):
        states = rates.shape[0]
        take(b, seg_s, enter_s, seg_s, False)
        take(b, seg_v, entering, seg_v, True)
        at = block_of(b)
        features_p[:, at] = jnp.zeros((POS, BLOCK, LANES), F32)
        steps_p[:, at] = jnp.zeros((POS, BLOCK, LANES), F32)

        def group(ns, d):
            r = [rates[n, d] for n in ns]
            vert = [[start_rows[n, j, d] for j in range(BJ)] for n in ns]
            from_v, from_s = [{} for _ in ns], [{} for _ in ns]
            exps = [{} for _ in ns]
            for i in range(BI):
                before = before_cols[i, d]
                state = [seg_s[n, i, d] * jnp.exp2(r[k] * before) for k, n in enumerate(ns)]
                for j in range(BJ):
                    p = i * BJ + j
                    c, s, g = step_p[p, d], source_p[p, d], grad_p[p, d]
                    for k, n in enumerate(ns):
                        m = c * r[k]
                        decay = jnp.exp2(m)
                        dv = decay * vert[k][j]
                        vert[k][j] = dv + s * row_of(write_p, p, n)
                        ds = decay * state[k]
                        state[k] = ds + vert[k][j]
                        sum_r[p, pl.ds(n * 8, 8)] += state[k] * g
                        from_v[k][p] = dv
                        from_s[k][p] = ds
                        exps[k][p] = m
            passed_v = [[None] * BJ for _ in ns]
            for j in range(BJ):
                after = before_rows[j, d]
                for i in range(BI):
                    after = after + step_p[i * BJ + j, d]
                for k, n in enumerate(ns):
                    passed_v[k][j] = seg_v[n, j, d] * jnp.exp2(-r[k] * after)
            total = [None for _ in ns]
            for i in reversed(range(BI)):
                passed = [start_cols[n, i, d] for n in ns]
                for j in reversed(range(BJ)):
                    p = i * BJ + j
                    s, g = source_p[p, d], grad_p[p, d]
                    sum_q, sum_t = None, None
                    for k, n in enumerate(ns):
                        adjoint = g * row_of(read_p, p, n) + passed[k]
                        m = exps[k][p]
                        decay = jnp.exp2(m)
                        passed[k] = decay * adjoint
                        adjoint_v = adjoint + passed_v[k][j]
                        passed_v[k][j] = decay * adjoint_v
                        q = (adjoint * from_s[k][p] + adjoint_v * from_v[k][p]) * m
                        total[k] = q if total[k] is None else total[k] + q
                        t = adjoint_v * row_of(write_p, p, n)
                        sum_q = q if sum_q is None else sum_q + q
                        sum_t = t if sum_t is None else sum_t + t
                        sum_w[p, pl.ds(n * 8, 8)] += adjoint_v * s
                    steps_p[p, d] += sum_q
                    features_p[p, d] += sum_t
            for k, n in enumerate(ns):
                decay_term[n, d] = total[k]

        each_group(b, states, 8, group)
        for p in range(POS):
            t, s = features_p[p, at], step_p[p, at]
            features_p[p, at] = s * t
            steps_p[p, at] = (source_p[p, at] * t + steps_p[p, at] * LN2) / s

    def last(self, step_p, source_p, grad_p, rates, start_rows, start_cols, seg_s, seg_v,
             enter_s, keep, got, write_p, read_p, rates_v, before_rows, before_cols, sum_rows,
             core, features_p, steps_p, sum_w, sum_r, grad_decay,
             entering, decay_term):
        for n in range(rates.shape[0]):
            out = lax.dot_general(
                jnp.ones((8, 2 * LANES), BF16), jnp.concatenate(halves(decay_term[n]), 1),
                (((1,), (1,)), ((), ())), preferred_element_type=F32,
            )
            grad_decay[pl.ds(n, 1)] = out[0:1] * LN2


class Unpack:
    def lead(self, i, features_p, steps_p, sum_w, sum_r, features, steps, writes, reads, turned):
        for j in range(BJ):
            for values, out in ((features_p, features), (steps_p, steps)):
                back = values[i * BJ + j].T
                for hs in range(HS):
                    out[hs, i, pl.ds(j, WS, stride=BJ), :] = back[hs * WS : hs * WS + WS]
        states = writes.shape[2]
        for values, out in ((sum_w, writes), (sum_r, reads)):
            for j in range(BJ):
                back = sum(values[i * BJ + j, pl.ds(k, states, stride=8), :] for k in range(8)).T
                for hs in range(HS):
                    turned[hs, pl.ds(j, WS, stride=BJ), :] = back[hs * WS : hs * WS + WS]
            for hs in range(HS):
                out[hs, i] = turned[hs].T


def prefix_kernel(held, sums, rates, out, *, reverse):
    size, share = out.shape[:2]
    at = sums.shape[1] - 1
    order = list(reversed(range(size))) if reverse else list(range(size))
    for n in range(share):
        before = jnp.zeros(out.shape[2:], F32)
        for k in order:
            out[k, n] = before
            before = jnp.exp2(rates[n] * sums[k, at]) * before + held[k, n]


def cut(ref, kind, k):
    if kind == "channels":
        index = (slice(None),) * (len(ref.shape) - 2) + (block_of(k),)
        return ref.at[index]
    if kind == "second":
        return ref.at[:, k]
    size = ref.shape[0] // BI
    return ref.at[pl.ds(k * size, size)]


def run(stage, ins, outs, scratch=(), micros=5):
    in_kinds, out_kinds = [k for _, k in ins], [k for _, k in outs]
    shapes = [a.shape for a, _ in ins] + [s for s, _ in outs]
    types = [a.dtype for a, _ in ins] + [F32 for _ in outs]
    kinds = in_kinds + out_kinds
    phase = {"whole": 0, "second": 1, "first": 1, "channels": 2}
    copied = [at for at, k in enumerate(kinds) if k in phase]
    count = len(ins)

    def kernel(*refs):
        given = list(refs[: len(kinds)])
        rest = refs[len(kinds) :]
        buffers, sems = rest[: len(copied)], rest[len(copied)]
        extra = rest[len(copied) + 1 :]
        views = list(given)
        into, out_of = [[], [], []], [[], [], []]
        for slot, at in enumerate(copied):
            views[at] = buffers[slot]

            def copy(k, slot=slot, at=at):
                far, near = given[at], buffers[slot]
                if kinds[at] != "whole":
                    far, near = cut(far, kinds[at], k), cut(near, kinds[at], k)
                pair = (far, near) if at < count else (near, far)
                return pltpu.make_async_copy(*pair, sems.at[slot, k])

            (into if at < count else out_of)[phase[kinds[at]]].append(copy)

        def part(which, name):
            def one(k, carry):
                for copy in into[which]:
                    copy(k).wait()
                getattr(stage, name)(k, *views, *extra)
                early = 1 if hasattr(stage, "after") else 0
                for copy in out_of[which][:early]:
                    copy(k).start()
                if early:
                    stage.after(k, *views, *extra)
                for copy in out_of[which][early:]:
                    copy(k).start()
                return carry

            lax.fori_loop(0, STEPS, one, 0)

        for which in range(3):
            for k in range(STEPS if which else 1):
                for copy in into[which]:
                    copy(k).start()
        for copy in into[0]:
            copy(0).wait()
        if hasattr(stage, "first"):
            stage.first(*views, *extra)
        if hasattr(stage, "lead"):
            part(1, "lead")
        if hasattr(stage, "main"):
            part(2, "main")
        if hasattr(stage, "last"):
            stage.last(*views, *extra)
        for copy in out_of[0]:
            copy(0).start()
        for which in range(3):
            for k in range(STEPS if which else 1):
                for copy in out_of[which]:
                    copy(k).wait()

    def spec(kind):
        if kind == "small":
            return pl.BlockSpec(memory_space=pltpu.VMEM)
        if kind == "scalar":
            return pl.BlockSpec(memory_space=pltpu.SMEM)
        return pl.BlockSpec(memory_space=pl.ANY)

    return pl.pallas_call(
        kernel,
        out_shape=[jax.ShapeDtypeStruct(s, F32) for s, _ in outs],
        in_specs=[spec(k) for k in in_kinds],
        out_specs=[spec(k) for k in out_kinds],
        scratch_shapes=[pltpu.VMEM(shapes[at], types[at]) for at in copied]
        + [pltpu.SemaphoreType.DMA((len(copied), STEPS))]
        + [pltpu.VMEM(s, F32) for s in scratch],
        compiler_params=pltpu.CompilerParams(vmem_limit_bytes=60 << 20),
        cost_estimate=pl.CostEstimate(
            flops=0, bytes_accessed=int(micros * 3.3e6), transcendentals=0
        ),
    )(*[a for a, _ in ins])


def swap_cores(x, size):
    return lax.ppermute(x, "row", [(k, k ^ 1) for k in range(size)])


def tied(*arrays):
    return lax.optimization_barrier(arrays)


def row_total(keep, give, sums, other_sums, rates, size, reverse):
    count = keep.shape[0]
    core = lax.axis_index("row") % 2
    theirs = swap_cores(give, size)
    rate = lax.dynamic_slice_in_dim(rates, core * count, count, 0)
    first = core == (1 if reverse else 0)
    near = jnp.where(first, keep, theirs)
    far = jnp.where(first, theirs, keep)
    near_sum = jnp.where(first, sums, other_sums)
    far_sum = jnp.where(first, other_sums, sums)
    total = far + jnp.exp2(rate * far_sum) * near
    return total, near, near_sum, far_sum, rate


def row_carry(total, near, near_sum, far_sum, rate, beside, size, reverse):
    core = lax.axis_index("row") % 2
    first = core == (1 if reverse else 0)
    sign = -2 if reverse else 2

    def shift(x, by):
        return lax.ppermute(
            x, "row", [(k, k + by) for k in range(size) if 0 <= k + by < size]
        )

    entering = shift(total, sign)
    if size > 4:
        span = shift(near_sum + far_sum, sign)
        by = sign
        while abs(by) < size - 2:
            entering = entering + jnp.exp2(rate * span) * shift(entering, by)
            span = span + shift(span, by)
            by *= 2
    entering, _ = tied(entering, beside)
    to_far = near + jnp.exp2(rate * near_sum) * entering
    keep = jnp.where(first, entering, to_far)
    give = jnp.where(first, to_far, entering)
    return keep, swap_cores(give, size)


def col_gather(sent):
    return lax.all_to_all(sent, "col", 0, 0)


def col_carry(held, sums, rates, reverse):
    size, share = held.shape[0], rates.shape[0]
    vmem = pl.BlockSpec(memory_space=pltpu.VMEM)
    return pl.pallas_call(
        functools.partial(prefix_kernel, reverse=reverse),
        out_shape=jax.ShapeDtypeStruct((size, share) + held.shape[2:], F32),
        in_specs=[vmem] * 3,
        out_specs=vmem,
        compiler_params=pltpu.CompilerParams(vmem_limit_bytes=4 << 20),
    )(held, sums, rates)


def col_return(carries):
    back = lax.all_to_all(carries, "col", 0, 0)
    return back.reshape((-1,) + carries.shape[2:])


def total_of(x, rows, cols):
    terms = [x] + [
        lax.ppermute(x, "row", [(k, k ^ by) for k in range(rows)]) for by in range(1, rows)
    ]
    while len(terms) > 1:
        terms = [a + b for a, b in zip(terms[::2], terms[1::2])]
    parts = lax.all_to_all(jnp.broadcast_to(terms[0][None], (cols,) + x.shape), "col", 0, 0)
    return jnp.sum(parts, 0)


def shards(features, step_size, write_weights, read_weights, decay_log, out_grad, sizes):
    rows, cols = sizes
    states = decay_log.shape[0]
    share = states // cols
    tile_h, tile_w = features.shape[:2]
    orders = {k: jnp.asarray(v, BF16) for k, v in lane_orders().items()}
    plane, quad = (POS, D, LANES), (4, D, LANES)
    seg = (states, 4, D, LANES)
    all_rates = (states, D, LANES)
    small = (POS, states, LANES)
    packed = (HS, BI, tile_w, D)
    weights = (HS, BI, states, tile_w)
    turned = (HS, tile_w, states)
    size_v, size_s = (states, D // 2, LANES), (states, D // 4, LANES)
    half_v = (states // 2,) + size_v[1:]
    core = (lax.axis_index("row") % 2).astype(jnp.int32).reshape(1)
    place = lax.axis_index("col").astype(jnp.int32).reshape(1)

    (step_p, grad_p, rates, seg_cols, read_p, rates_v, rates_s, own_rates, before_cols, sum_cols,
     sum_rows, sent) = run(
        AdjointCols(),
        [(step_size.reshape(packed), "second"), (out_grad.reshape(packed), "second"),
         (read_weights.swapaxes(1, 2).reshape(weights), "second"),
         (decay_log.reshape(BI, states // BI, D), "small"), (place, "scalar"),
         (orders["left"], "whole"), (orders["right"], "whole")],
        [(plane, "first"), (plane, "first"), (all_rates, "first"), (seg, "channels"),
         (small, "whole"), (size_v, "whole"), (size_s, "whole"), ((share,) + size_s[1:], "whole"),
         (quad, "whole"), (size_s[1:], "whole"), (size_v[1:], "whole"),
         ((cols, share + 1) + size_s[1:], "whole")],
        [turned, size_s],
    )
    held = col_gather(sent)
    other_rows = swap_cores(sum_rows, rows)
    step_p, _ = tied(step_p, sent)
    source_p, seg_rows, write_p, before_rows, keep, give = run(
        ForwardRows(),
        [(features.reshape(packed), "second"), (step_p, "first"), (rates, "channels"),
         (write_weights.swapaxes(1, 2).reshape(weights), "second"), (rates_v, "whole"),
         (sum_rows, "whole"), (core, "scalar"), (orders["above"], "whole")],
        [(plane, "first"), (seg, "channels"), (small, "whole"), (quad, "whole"),
         (half_v, "whole"), (half_v, "whole")],
        [turned, size_v],
    )
    total = row_total(keep, give, sum_rows, other_rows, rates_v, rows, False)
    held, first = tied(held, total[0])
    col_sums = held
    carries = col_carry(held, held, own_rates, True)
    enter_cols = col_return(carries)
    keep, got = row_carry(first, *total[1:], carries, rows, False)
    start_rows, seg_s, leave_s = run(
        ForwardCols(),
        [(step_p, "channels"), (source_p, "channels"), (rates, "channels"),
         (seg_rows, "channels"), (keep, "whole"), (got, "whole"), (write_p, "whole"),
         (rates_s, "whole"), (before_rows, "whole"), (before_cols, "whole"),
         (sum_cols, "whole"), (core, "scalar"), (orders["left"], "whole")],
        [(seg, "channels"), (seg, "channels"), (size_s, "whole")], [size_v], 10,
    )
    held = col_gather(leave_s.reshape((cols, share) + size_s[1:]))
    enter_cols, _ = tied(enter_cols, leave_s)
    start_cols, seg_v, keep, give = run(
        AdjointRows(),
        [(step_p, "channels"), (grad_p, "channels"), (rates, "channels"),
         (seg_cols, "channels"), (enter_cols, "whole"), (read_p, "whole"), (rates_s, "whole"),
         (before_rows, "whole"), (before_cols, "whole"), (sum_cols, "whole"), (core, "scalar"),
         (orders["below"], "whole")],
        [(seg, "channels"), (seg, "channels"), (half_v, "whole"), (half_v, "whole")],
        [size_s, size_v], 10,
    )
    held, give = tied(held, give)
    total = row_total(keep, give, sum_rows, other_rows, rates_v, rows, True)
    held, first = tied(held, total[0])
    carries = col_carry(held, col_sums, own_rates, False)
    enter_s = col_return(carries)
    keep, got = row_carry(first, *total[1:], carries, rows, True)
    features_p, steps_p, sum_w, sum_r, grad_decay = run(
        Final(),
        [(step_p, "channels"), (source_p, "channels"), (grad_p, "channels"),
         (rates, "channels"), (start_rows, "channels"), (start_cols, "channels"),
         (seg_s, "channels"), (seg_v, "channels"), (enter_s, "whole"), (keep, "whole"),
         (got, "whole"), (write_p, "whole"), (read_p, "whole"), (rates_v, "whole"),
         (before_rows, "whole"), (before_cols, "whole"), (sum_rows, "whole"), (core, "scalar")],
        [(plane, "channels"), (plane, "channels"), ((POS, states * 8, LANES), "whole"),
         ((POS, states * 8, LANES), "whole"), ((states, D), "whole")],
        [size_v, all_rates], 25,
    )
    grad_decay = total_of(grad_decay, rows, cols)
    grad_features, grad_step, grad_write, grad_read = run(
        Unpack(),
        [(features_p, "first"), (steps_p, "first"), (sum_w, "first"), (sum_r, "first")],
        [(packed, "second"), (packed, "second"), (weights, "second"), (weights, "second")],
        [turned],
    )
    weights = (tile_h, states, tile_w)
    return (
        grad_features.reshape(features.shape),
        grad_step.reshape(features.shape),
        grad_write.reshape(weights).swapaxes(1, 2),
        grad_read.reshape(weights).swapaxes(1, 2),
        grad_decay,
    )


def solution(mesh):
    spec = P("row", "col", None)
    sizes = (mesh.shape["row"], mesh.shape["col"])
    return jax.shard_map(
        functools.partial(shards, sizes=sizes),
        mesh=mesh,
        in_specs=(spec, spec, spec, spec, P(), spec),
        out_specs=(spec, spec, spec, spec, P()),
        check_vma=False,
    )
```
